512 devices in a mesh: dp: 32 (over x, z), tensor: 4 (over y_lo), group: 4 (over y_hi, core).
Axes of the slice: x: 4, y: 8 (y_hi: 2, y_lo: 4; y = y_hi * 4 + y_lo), z: 8, core: 2. Of those that a mesh axis runs over, the one named last changes fastest.
Arguments:
- image_in: bfloat16 [128, 256, 1408], P(('dp', 'group')), may hold values from -6 to 6
- enc_gain: float32 [1408], replicated, may hold values from 0.1 to 1.9
- enc_up: bfloat16 [1408, 4096], P('group', 'tensor'), may hold values from -0.15625 to 0.15625
- enc_down: bfloat16 [4096, 1408], P('tensor', 'group'), may hold values from -0.09375 to 0.09375
- text_in: bfloat16 [128, 128, 2048], P('dp', ('tensor', 'group')), may hold values from -6 to 6
- query_gain: float32 [2048], replicated, may hold values from 0.5 to 2
- w_query: bfloat16 [2048, 2048], P(None, ('tensor', 'group')), may hold values from -0.125 to 0.125
- w_key: bfloat16 [1408, 2048], P(None, ('tensor', 'group')), may hold values from -0.15625 to 0.15625
- w_value: bfloat16 [1408, 2048], P(None, ('tensor', 'group')), may hold values from -0.15625 to 0.15625
- w_out: bfloat16 [2048, 2048], P(('tensor', 'group')), may hold values from -0.125 to 0.125
- cotangent: bfloat16 [128, 128, 2048], P('dp', ('tensor', 'group')), may hold values from -6 to 6
Outputs:
- image_grad: bfloat16 [128, 256, 1408], P(('dp', 'group'))
- key_grad: float32 [1408, 2048], P('dp', ('tensor', 'group'))
- value_grad: float32 [1408, 2048], P('dp', ('tensor', 'group'))
The draws below stay inside these ranges and needn't reach their ends.
All inputs are finite; a program needn't handle non-finite values.
Results may differ from the reference program's by a relative error of at most 0.035.
Values may be sent and summed in bfloat16 or wider, within the bound.
No kernel may reach another device: no remote copies, remote signals or barrier semaphores. Data moves between devices by JAX's collectives and lax.ppermute only.
A program may use at most 64 MiB of HBM per device.

```python
import jax
import jax.numpy as jnp
from jax import lax

D_ENC = 1408
FF_ENC = 4096
D_DEC = 2048
HEADS = 16
HEAD_DIM = 128
PATCHES = 256
TEXT_LEN = 128
IMAGES = 128
N_DP = 32
N_TENSOR = 4
N_GROUP = 4


def draw_query_gain(key, part):
    key = jax.random.fold_in(key, 7)
    return jax.random.uniform(key, (D_DEC,), jnp.float32, 0.5, 1.5)


def steps_of(own_key, extent, shards, low, top_value):
    factor_of, own = 1.0, jax.random.fold_in(own_key, 6)
    for position, blocks in shards:
        heights = jnp.exp(jax.random.uniform(jax.random.fold_in(own, position), (blocks,), jnp.float32, low / len(shards), top_value / len(shards)))
        factor_of = factor_of * jnp.repeat(heights, extent[position] // blocks).reshape([-1 if axis == position else 1 for axis in range(len(extent))])
    return factor_of


def scatter_about(key, shape, width, most, pieces=(), dtype=jnp.bfloat16):
    drawn = width * jax.random.normal(key, shape, jnp.float32)
    if pieces:
        drawn = drawn * steps_of(key, shape, pieces, -0.22, 0.18)
    return jnp.clip(drawn, -most, most).astype(dtype)


def setup_inputs(seed: int = 0) -> dict:
    arg_keys = jax.random.split(jax.random.key(seed), 12)
    return {
        "image_in": scatter_about(arg_keys[0], (IMAGES, PATCHES, D_ENC), 1.0, 6.0, ((0, 128),)),
        "enc_gain": jnp.clip(1.0 + 0.18 * jax.random.normal(arg_keys[1], (D_ENC,), jnp.float32), 0.1, 1.9),
        "enc_up": scatter_about(arg_keys[2], (D_ENC, FF_ENC), D_ENC ** -0.5, 0.15625, ((0, 4), (1, 4))),
        "enc_down": scatter_about(arg_keys[3], (FF_ENC, D_ENC), FF_ENC ** -0.5, 0.09375, ((0, 4), (1, 4))),
        "text_in": scatter_about(arg_keys[4], (IMAGES, TEXT_LEN, D_DEC), 1.0, 6.0, ((0, 32), (1, 16))),
        "query_gain": draw_query_gain(jax.random.fold_in(arg_keys[11], 71), 0),
        "w_query": scatter_about(arg_keys[6], (D_DEC, HEADS * HEAD_DIM), D_DEC ** -0.5, 0.125, ((1, 16),)),
        "w_key": scatter_about(arg_keys[7], (D_ENC, HEADS * HEAD_DIM), D_ENC ** -0.5, 0.15625, ((1, 16),)),
        "w_value": scatter_about(arg_keys[8], (D_ENC, HEADS * HEAD_DIM), D_ENC ** -0.5, 0.15625, ((1, 16),)),
        "w_out": scatter_about(arg_keys[9], (HEADS * HEAD_DIM, D_DEC), (HEADS * HEAD_DIM) ** -0.5, 0.125, ((0, 16),)),
        "cotangent": scatter_about(arg_keys[10], (IMAGES, TEXT_LEN, D_DEC), 1.0, 6.0, ((0, 32), (1, 16))),
    }


EPSILON = 1e-06

def layer_norm(values, gain):
    floats = values.astype(jnp.float32)
    centre = lax.optimization_barrier(jnp.mean(floats, axis=-1, keepdims=True))
    spread = lax.optimization_barrier(jnp.mean(jnp.square(floats - centre), axis=-1, keepdims=True))
    inverse = lax.rsqrt(spread + EPSILON)
    normal = (floats - centre) * inverse
    return (normal * gain, normal, inverse)

def gelu_tanh(values):
    return jax.nn.gelu(values, approximate=True)

def rounded(values):
    return lax.optimization_barrier(values.astype(jnp.bfloat16)).astype(jnp.float32)

def reference(image_in, enc_gain, enc_up, enc_down, text_in, query_gain, w_query, w_key, w_value, w_out, cotangent):
    flat_in = image_in.reshape(-1, D_ENC)
    scaled, normal, inverse = layer_norm(flat_in, enc_gain)
    normed = scaled.astype(jnp.bfloat16)
    pre_act = jnp.dot(normed, enc_up, preferred_element_type=jnp.float32)
    activated = gelu_tanh(pre_act).astype(jnp.bfloat16)
    span = FF_ENC // N_TENSOR
    branch = jnp.zeros((flat_in.shape[0], D_ENC), jnp.float32)
    for block in range(N_TENSOR):
        part = jnp.dot(activated[:, block * span:(block + 1) * span], enc_down[block * span:(block + 1) * span], preferred_element_type=jnp.float32)
        branch = branch + rounded(part)
    encoded = (flat_in.astype(jnp.float32) + branch).astype(jnp.bfloat16).reshape(IMAGES, PATCHES, D_ENC)
    text_scaled, text_normal, text_inverse = layer_norm(text_in, query_gain)
    text_normed = text_scaled.astype(jnp.bfloat16)
    groups = N_TENSOR * N_GROUP
    columns = HEADS * HEAD_DIM // groups
    heads_here = HEADS // groups
    query_parts = jnp.transpose(w_query.reshape(D_DEC, groups, columns), (1, 0, 2))
    key_parts = jnp.transpose(w_key.reshape(D_ENC, groups, columns), (1, 0, 2))
    value_parts = jnp.transpose(w_value.reshape(D_ENC, groups, columns), (1, 0, 2))
    out_parts = w_out.reshape(groups, columns, D_DEC)

    def one_group(total, weights):
        part_query, part_key, part_value, part_out = weights
        query = (jnp.dot(text_normed.reshape(-1, D_DEC), part_query, preferred_element_type=jnp.float32) * HEAD_DIM ** (-0.5)).astype(jnp.bfloat16)
        query = query.reshape(IMAGES, TEXT_LEN, heads_here, HEAD_DIM)
        pair_weight = jnp.concatenate([part_key, part_value], axis=1)
        key_value = jnp.dot(encoded.reshape(-1, D_ENC), pair_weight, preferred_element_type=jnp.float32).astype(jnp.bfloat16)
        key_value = key_value.reshape(IMAGES, PATCHES, 2, heads_here, HEAD_DIM)
        keys = key_value[:, :, 0]
        values = key_value[:, :, 1]
        d_attn = jnp.dot(cotangent.reshape(-1, D_DEC), part_out.T, preferred_element_type=jnp.float32).astype(jnp.bfloat16)
        d_attn = d_attn.reshape(IMAGES, TEXT_LEN, heads_here, HEAD_DIM)
        scores = jnp.einsum('ithe,iphe->ihtp', query.astype(jnp.float32), keys.astype(jnp.float32))
        top = lax.optimization_barrier(jnp.max(scores, axis=-1, keepdims=True))
        expo = jnp.exp(scores - top)
        probs = expo / lax.optimization_barrier(jnp.sum(expo, axis=-1, keepdims=True))
        d_probs = jnp.einsum('ithe,iphe->ihtp', d_attn.astype(jnp.float32), values.astype(jnp.float32))
        d_scores = (probs * (d_probs - lax.optimization_barrier(jnp.sum(probs * d_probs, axis=-1, keepdims=True)))).astype(jnp.bfloat16)
        probs_low = probs.astype(jnp.bfloat16)
        d_keys = jnp.einsum('ihtp,ithe->iphe', d_scores.astype(jnp.float32), query.astype(jnp.float32)).astype(jnp.bfloat16)
        d_values = jnp.einsum('ihtp,ithe->iphe', probs_low.astype(jnp.float32), d_attn.astype(jnp.float32)).astype(jnp.bfloat16)
        d_pair = jnp.stack([d_keys, d_values], axis=2).reshape(IMAGES, PATCHES, 2 * columns)
        term = jnp.dot(d_pair.reshape(-1, 2 * columns), pair_weight.T, preferred_element_type=jnp.float32)
        total = total + rounded(term)
        block_terms = jnp.einsum('bipd,bipc->bdc', encoded.reshape(N_DP, -1, PATCHES, D_ENC).astype(jnp.float32), d_pair.reshape(N_DP, -1, PATCHES, 2 * columns).astype(jnp.float32))
        weight_sum = lax.optimization_barrier(jnp.sum(rounded(block_terms), axis=0))
        return (total, weight_sum)
    start_total = jnp.zeros((IMAGES * PATCHES, D_ENC), jnp.float32)
    total, weight_sums = lax.scan(one_group, start_total, (query_parts, key_parts, value_parts, out_parts))
    key_grad = jnp.transpose(weight_sums[:, :, :columns], (1, 0, 2)).reshape(D_ENC, HEADS * HEAD_DIM)
    value_grad = jnp.transpose(weight_sums[:, :, columns:], (1, 0, 2)).reshape(D_ENC, HEADS * HEAD_DIM)
    d_encoded = total.astype(jnp.bfloat16)
    d_act = jnp.dot(d_encoded, enc_down.T, preferred_element_type=jnp.float32)
    d_pre = jax.vjp(gelu_tanh, pre_act)[1](d_act)[0].astype(jnp.bfloat16)
    d_normed = jnp.zeros((flat_in.shape[0], D_ENC), jnp.float32)
    for block in range(N_TENSOR):
        part = jnp.dot(d_pre[:, block * span:(block + 1) * span], enc_up[:, block * span:(block + 1) * span].T, preferred_element_type=jnp.float32)
        d_normed = d_normed + rounded(part)
    scaled_grad = d_normed * enc_gain
    d_input = inverse * (scaled_grad - lax.optimization_barrier(jnp.mean(scaled_grad, axis=-1, keepdims=True)) - normal * lax.optimization_barrier(jnp.mean(scaled_grad * normal, axis=-1, keepdims=True)))
    image_grad = (d_encoded.astype(jnp.float32) + d_input).astype(jnp.bfloat16).reshape(IMAGES, PATCHES, D_ENC)
    return (image_grad, key_grad, value_grad)
```

```python
import jax
import jax.numpy as jnp
from jax import lax
from jax.sharding import Mesh, PartitionSpec as P

HEAD_DIM = 128
EPSILON = 1e-06
BF = jnp.bfloat16
F32 = jnp.float32


def layer_norm(values, gain):
    floats = values.astype(F32)
    centre = jnp.mean(floats, axis=-1, keepdims=True)
    spread = jnp.mean(jnp.square(floats - centre), axis=-1, keepdims=True)
    inverse = lax.rsqrt(spread + EPSILON)
    normal = (floats - centre) * inverse
    return (normal * gain, normal, inverse)


def gelu_tanh(values):
    return jax.nn.gelu(values, approximate=True)


def shift(value, axis, by):
    size = lax.axis_size(axis)
    return lax.ppermute(value, axis, [(i, (i + by) % size) for i in range(size)])


def swap(value, axis, bit=1):
    size = lax.axis_size(axis)
    return lax.ppermute(value, axis, [(i, i ^ bit) for i in range(size)])


def rows_at(value, start, size):
    return lax.dynamic_slice_in_dim(value, start, size, axis=0)


def put(buffer, block, start):
    return lax.dynamic_update_slice_in_dim(buffer, block, start, axis=0)


def far_block(own, axis):
    quarter = own.shape[0] // 4
    mine = lax.rem(lax.axis_index(axis), 4)
    piece = swap(rows_at(own, mine * quarter, quarter), "yh")
    pieces = [piece, shift(piece, axis, -1), shift(piece, axis, 2), shift(piece, axis, 1)]
    block = jnp.zeros_like(own)
    for offset, part in enumerate(pieces):
        block = put(block, part, lax.rem(mine + offset, 4) * quarter)
    return block


def group_blocks(own, axis):
    far = far_block(own, axis)
    return own, far, swap(own, "core"), swap(far, "core")


def stacked(blocks, group):
    own, far, near, far_near = blocks
    rows = own.shape[0]
    buffer = jnp.zeros((4 * rows, own.shape[1]), own.dtype)
    buffer = put(buffer, own, group * rows)
    buffer = put(buffer, near, (group ^ 1) * rows)
    buffer = put(buffer, far, (group ^ 2) * rows)
    return put(buffer, far_near, (group ^ 3) * rows)


def scatter_sum(partial, axis):
    size = lax.axis_size(axis)
    rows = partial.shape[0] // size
    here = lax.axis_index(axis)
    total = rows_at(partial, here * rows, rows).astype(F32)
    for by in range(1, size):
        block = rows_at(partial, lax.rem(here + by, size) * rows, rows)
        total = total + shift(block, axis, by).astype(F32)
    return total


def gather_rows(block, axis):
    size = lax.axis_size(axis)
    rows = block.shape[0]
    here = lax.axis_index(axis)
    whole = jnp.zeros((size * rows,) + block.shape[1:], block.dtype)
    whole = put(whole, block, here * rows)
    for by in range(1, size):
        whole = put(whole, shift(block, axis, by), lax.rem(here - by + size, size) * rows)
    return whole


def halved(partial, axis, bit):
    half = partial.shape[0] // 2
    side = (lax.axis_index(axis) // bit) % 2
    sent = rows_at(partial, (1 - side) * half, half).astype(BF)
    return rows_at(partial, side * half, half) + swap(sent, axis, bit).astype(F32)


def local(
    image_in, enc_gain, enc_up, enc_down, text_in, query_gain, w_query, w_key, w_value, w_out, cotangent
):
    _, patches, width = image_in.shape
    group = lax.axis_index("yh") * 2 + lax.axis_index("core")
    tensor = lax.axis_index("tensor")
    flat_in = image_in.reshape(patches, width)

    up = stacked(group_blocks(enc_up, "x"), group)
    down = stacked(group_blocks(enc_down.T, "z"), group)
    packed = jnp.concatenate([w_key, w_value, w_query, w_out.T], axis=0)
    heads = group_blocks(packed, "x")
    dec = w_query.shape[0]
    pair_weight = jnp.concatenate(
        [part for block in heads for part in (block[:width], block[width : 2 * width])], axis=1
    )
    query_weight = jnp.concatenate([block[2 * width : 2 * width + dec] for block in heads], axis=1)
    out_weight = jnp.concatenate([block[2 * width + dec :] for block in heads], axis=1)

    text_normed = layer_norm(text_in, query_gain)[0].astype(BF)
    both = jnp.stack([text_normed, cotangent], axis=1)
    per = 2 * text_in.shape[1] * dec
    rows = text_in.shape[1]
    group_rows = []
    for other in range(4):
        block = lax.dynamic_index_in_dim(both, group ^ other, axis=0, keepdims=False)
        if other:
            pairs = [(i, i ^ other) for i in range(4)]
            block = lax.ppermute(block, ("yh", "core"), pairs)
        group_rows.append(block)
    caption = jnp.concatenate(group_rows, axis=1).reshape(2, 4 * rows, dec)
    caption = gather_rows(caption.reshape(1, 2, 4 * rows, dec), "tensor")
    text_mine = caption[:, 0].reshape(-1, dec)
    cot_mine = caption[:, 1].reshape(-1, dec)

    scaled, _, _ = layer_norm(flat_in, enc_gain)
    normed = scaled.astype(BF)
    pre_act = jnp.dot(normed, up, preferred_element_type=F32)
    activated = gelu_tanh(pre_act).astype(BF)
    branch_part = lax.dot_general(
        activated, down, (((1,), (1,)), ((), ())), preferred_element_type=F32
    ).astype(BF)
    own_rows = patches // lax.axis_size("tensor")
    in_rows = rows_at(flat_in, tensor * own_rows, own_rows)
    encoded_rows = (in_rows.astype(F32) + scatter_sum(branch_part, "tensor")).astype(BF)
    encoded = gather_rows(encoded_rows, "tensor")

    query = (
        jnp.dot(text_mine, query_weight, preferred_element_type=F32) * HEAD_DIM ** (-0.5)
    ).astype(BF)
    d_attn = jnp.dot(cot_mine, out_weight, preferred_element_type=F32).astype(BF)
    query = query.reshape(-1, 4, HEAD_DIM)
    d_attn = d_attn.reshape(-1, 4, HEAD_DIM)
    key_value = jnp.dot(encoded, pair_weight, preferred_element_type=F32).astype(BF)
    key_value = key_value.reshape(patches, 4, 2, HEAD_DIM)
    keys, values = key_value[:, :, 0], key_value[:, :, 1]
    scores = jnp.einsum("the,phe->htp", query, keys, preferred_element_type=F32)
    top = jnp.max(scores, axis=-1, keepdims=True)
    expo = jnp.exp(scores - top)
    probs = expo / jnp.sum(expo, axis=-1, keepdims=True)
    d_probs = jnp.einsum("the,phe->htp", d_attn, values, preferred_element_type=F32)
    d_scores = (probs * (d_probs - jnp.sum(probs * d_probs, axis=-1, keepdims=True))).astype(BF)
    probs_low = probs.astype(BF)
    d_keys = jnp.einsum("htp,the->phe", d_scores, query, preferred_element_type=F32).astype(BF)
    d_values = jnp.einsum("htp,the->phe", probs_low, d_attn, preferred_element_type=F32).astype(BF)
    d_pair = jnp.stack([d_keys, d_values], axis=2).reshape(patches, 8 * HEAD_DIM)

    term = lax.dot_general(
        d_pair, pair_weight, (((1,), (1,)), ((), ())), preferred_element_type=F32
    ).astype(BF)
    grad_rows = scatter_sum(term, "tensor").astype(BF)
    flat_grad = gather_rows(grad_rows, "tensor")

    pair_cols = 2 * HEAD_DIM
    keep = lax.dot_general(
        encoded, d_pair[:, : 2 * pair_cols], (((0,), (0,)), ((), ())), preferred_element_type=F32
    )
    give = lax.dot_general(
        encoded, d_pair[:, 2 * pair_cols :], (((0,), (0,)), ((), ())), preferred_element_type=F32
    ).astype(BF)
    sums = (keep + swap(give, "core").astype(F32)).astype(BF)
    sums = scatter_sum(sums, "x")
    sums = sums[:, :pair_cols] + swap(sums[:, pair_cols:].astype(BF), "yh").astype(F32)
    sums = sums.reshape(8, -1, pair_cols)
    for bit in (4, 2, 1):
        sums = halved(sums, "z", bit)
    sums = sums[0]
    key_grad, value_grad = sums[:, :HEAD_DIM], sums[:, HEAD_DIM:]

    d_act = jnp.dot(flat_grad, down, preferred_element_type=F32)
    d_pre = jax.vjp(gelu_tanh, pre_act)[1](d_act)[0].astype(BF)
    d_norm_part = lax.dot_general(
        d_pre, up, (((1,), (1,)), ((), ())), preferred_element_type=F32
    ).astype(BF)
    d_normed = scatter_sum(d_norm_part, "tensor")
    _, normal, inverse = layer_norm(in_rows, enc_gain)
    scaled_grad = d_normed * enc_gain
    d_input = inverse * (
        scaled_grad
        - jnp.mean(scaled_grad, axis=-1, keepdims=True)
        - normal * jnp.mean(scaled_grad * normal, axis=-1, keepdims=True)
    )
    image_rows = (grad_rows.astype(F32) + d_input).astype(BF)
    image_grad = gather_rows(image_rows, "tensor").reshape(1, patches, width)
    return (image_grad, key_grad, value_grad)


def solution(mesh):
    fine = Mesh(mesh.devices.reshape(4, 8, 4, 2, 2), ("x", "z", "tensor", "yh", "core"))
    dp, group, heads = ("x", "z"), ("yh", "core"), ("tensor", "yh", "core")
    in_specs = (
        P(dp + group, None, None),
        P(),
        P(group, "tensor"),
        P("tensor", group),
        P(dp, heads, None),
        P(),
        P(None, heads),
        P(None, heads),
        P(None, heads),
        P(heads, None),
        P(dp, heads, None),
    )
    out_specs = (P(dp + group, None, None), P(dp, heads), P(dp, heads))
    return jax.shard_map(local, mesh=fine, in_specs=in_specs, out_specs=out_specs, check_vma=False)
```

```python
import functools

import jax
import jax.numpy as jnp
from jax import lax
from jax.experimental import pallas as pl
from jax.experimental.pallas import tpu as pltpu
from jax.sharding import Mesh, PartitionSpec as P

HEAD_DIM = 128
EPSILON = 1e-06
BF = jnp.bfloat16
F32 = jnp.float32
PARTS = 4
PARAMS = pltpu.CompilerParams(vmem_limit_bytes=48 * 1024 * 1024)
VMEM = pl.BlockSpec(memory_space=pltpu.VMEM)
ANY = pl.BlockSpec(memory_space=pl.ANY)
SMEM = pl.BlockSpec(memory_space=pltpu.SMEM)
LAST = (((1,), (1,)), ((), ()))


def layer_norm(values, gain):
    floats = values.astype(F32)
    centre = jnp.mean(floats, axis=-1, keepdims=True)
    spread = jnp.mean(jnp.square(floats - centre), axis=-1, keepdims=True)
    inverse = lax.rsqrt(spread + EPSILON)
    normal = (floats - centre) * inverse
    return (normal * gain, normal, inverse)


def gelu_pair(values):
    c = 0.7978845608028654
    square = values * values
    tanh = jnp.tanh(c * values * (1.0 + 0.044715 * square))
    half = 0.5 * (1.0 + tanh)
    slope = half + 0.5 * values * (1.0 - tanh * tanh) * c * (1.0 + 3 * 0.044715 * square)
    return values * half, slope


def dot(a, b):
    return jnp.dot(a, b, preferred_element_type=F32)


def dot_last(a, b):
    return lax.dot_general(a, b, LAST, preferred_element_type=F32)


def block_copies(place, blocks, whole, sems):
    rows = blocks[0].shape[0]
    group = place[0]
    copies = []
    for bits, block in enumerate(blocks):
        start = pl.multiple_of((group ^ bits) * rows, 16)
        copies.append(pltpu.make_async_copy(block, whole.at[pl.ds(start, rows)], sems.at[bits]))
    return copies


def up_kernel(place, image, gain, u0, u1, u2, u3, act, slope, in_rows, up, rows4, sems, row_sems):
    copies = block_copies(place, (u0, u1, u2, u3), up, sems)
    rows = in_rows.shape[0]
    moves = []
    for k in range(PARTS):
        start = pl.multiple_of(lax.rem(place[1] + PARTS - k, PARTS) * rows, 16)
        moves.append(
            pltpu.make_async_copy(
                image.at[pl.ds(start, rows)], rows4.at[pl.ds(k * rows, rows)], row_sems.at[k]
            )
        )
    for copy in moves + copies:
        copy.start()
    for copy in moves:
        copy.wait()
    in_rows[...] = rows4[pl.ds(0, rows)]
    normed = layer_norm(rows4[...], gain[...])[0].astype(BF)
    for copy in copies:
        copy.wait()
    for n in range(4):
        cols = pl.ds(n * 256, 256)
        value, grad = gelu_pair(dot(normed, up[:, cols]))
        act[:, cols] = value.astype(BF)
        slope[:, cols] = grad


def down_kernel(place, act, d0, d1, d2, d3, o0, o1, o2, o3, down, sems):
    copies = block_copies(place, (d0, d1, d2, d3), down, sems)
    for copy in copies:
        copy.start()
    for copy in copies:
        copy.wait()
    split_rows(dot_last(act[...], down[...]).astype(BF), (o0, o1, o2, o3))


def split_rows(value, outs):
    rows = outs[0].shape[0]
    for k, out in enumerate(outs):
        out[...] = value[k * rows : (k + 1) * rows]


def query_kernel(caption, p0, p1, p2, p3, query, d_attn, w, sems):
    dec = caption.shape[-1]
    skip = p0.shape[1] - dec
    copies = [
        pltpu.make_async_copy(p.at[:, pl.ds(skip, dec)], w.at[k], sems.at[k])
        for k, p in enumerate((p0, p1, p2, p3))
    ]
    for copy in copies:
        copy.start()
    text = caption[:, 0].reshape(-1, dec)
    cot = caption[:, 1].reshape(-1, dec)
    for k, copy in enumerate(copies):
        copy.wait()
        query[k] = (dot_last(text, w[k, :HEAD_DIM]) * HEAD_DIM ** (-0.5)).astype(BF)
        d_attn[k] = dot_last(cot, w[k, HEAD_DIM:]).astype(BF)


def attention_kernel(
    e0, e1, e2, e3, query, d_attn, p0, p1, p2, p3, o0, o1, o2, o3, encoded, d_pair, w, sems
):
    width = e0.shape[1]
    copies = [
        pltpu.make_async_copy(p.at[:, pl.ds(0, width)], w.at[k], sems.at[k])
        for k, p in enumerate((p0, p1, p2, p3))
    ]
    for copy in copies:
        copy.start()
    rows = e0.shape[0]
    for k, e in enumerate((e0, e1, e2, e3)):
        encoded[pl.ds(k * rows, rows)] = e[...]
    tokens = encoded[...]
    term = None
    for k, copy in enumerate(copies):
        copy.wait()
        pair = dot_last(tokens, w[k]).astype(BF)
        keys, values = pair[:, :HEAD_DIM], pair[:, HEAD_DIM:]
        q, da = query[k], d_attn[k]
        scores = dot_last(keys, q)
        expo = jnp.exp(scores - jnp.max(scores, axis=0, keepdims=True))
        probs = expo / jnp.sum(expo, axis=0, keepdims=True)
        d_probs = dot_last(values, da)
        mean = jnp.sum(probs * d_probs, axis=0, keepdims=True)
        d_scores = (probs * (d_probs - mean)).astype(BF)
        d_keys = dot(d_scores, q).astype(BF)
        d_values = dot(probs.astype(BF), da).astype(BF)
        grads = jnp.concatenate([d_keys, d_values], axis=1)
        d_pair[:, pl.ds(k * 2 * HEAD_DIM, 2 * HEAD_DIM)] = grads
    for k in range(PARTS):
        part = dot(d_pair[:, pl.ds(k * 2 * HEAD_DIM, 2 * HEAD_DIM)], w[k])
        term = part if term is None else term + part
    split_rows(term.astype(BF), (o0, o1, o2, o3))


def back_kernel(
    place, g0, g1, g2, g3, slope, d0, d1, d2, d3, u0, u1, u2, u3,
    o0, o1, o2, o3, down, up, grads, d_pre, down_sems, up_sems,
):
    first = block_copies(place, (d0, d1, d2, d3), down, down_sems)
    second = block_copies(place, (u0, u1, u2, u3), up, up_sems)
    for copy in first + second:
        copy.start()
    rows = g0.shape[0]
    for k, g in enumerate((g0, g1, g2, g3)):
        grads[pl.ds(k * rows, rows)] = g[...]
    for copy in first:
        copy.wait()
    for n in range(4):
        cols = pl.ds(n * 256, 256)
        d_pre[:, cols] = (dot(grads[...], down[:, cols]) * slope[:, cols]).astype(BF)
    for copy in second:
        copy.wait()
    split_rows(dot_last(d_pre[...], up[...]).astype(BF), (o0, o1, o2, o3))


def shift(value, axis, by):
    size = lax.axis_size(axis)
    return lax.ppermute(value, axis, [(i, (i + by) % size) for i in range(size)])


def swap(value, axis, bit=1):
    size = lax.axis_size(axis)
    return lax.ppermute(value, axis, [(i, i ^ bit) for i in range(size)])


def rows_at(value, start, size):
    return lax.dynamic_slice_in_dim(value, start, size, axis=0)


def after(value, *others):
    return lax.optimization_barrier((value,) + others)[0]


def far_block(own, axis):
    quarter = own.shape[0] // PARTS
    piece = swap(rows_at(own, lax.axis_index(axis) * quarter, quarter), "yh")
    return lax.all_gather(piece, axis, axis=0, tiled=True)


def group_blocks(own, axis):
    far = far_block(own, axis)
    return own, swap(own, "core"), far, swap(far, "core")


def sum_blocks(blocks):
    total = blocks[0].astype(F32)
    for by in range(1, PARTS):
        total = total + shift(blocks[PARTS - by], "tensor", by).astype(F32)
    return total


def gather_blocks(block):
    return [block] + [shift(block, "tensor", by) for by in range(1, PARTS)]


def scatter_sum(partial, axis):
    size = lax.axis_size(axis)
    rows = partial.shape[0] // size
    here = lax.axis_index(axis)
    total = rows_at(partial, here * rows, rows).astype(F32)
    for by in range(1, size):
        block = rows_at(partial, lax.rem(here + by, size) * rows, rows)
        total = total + shift(block, axis, by).astype(F32)
    return total


def halved(partial, axis, bit):
    half = partial.shape[0] // 2
    side = (lax.axis_index(axis) // bit) % 2
    sent = rows_at(partial, (1 - side) * half, half).astype(BF)
    return rows_at(partial, side * half, half) + swap(sent, axis, bit).astype(F32)


def local(
    image_in, enc_gain, enc_up, enc_down, text_in, query_gain, w_query, w_key, w_value, w_out, cotangent
):
    _, patches, width = image_in.shape
    group = lax.axis_index("yh") * 2 + lax.axis_index("core")
    tensor = lax.axis_index("tensor")
    place = jnp.stack([group, tensor]).astype(jnp.int32)
    flat_in = image_in.reshape(patches, width)
    rows = patches // PARTS
    hidden = enc_up.shape[1]
    dec = w_query.shape[0]
    shape = jax.ShapeDtypeStruct
    row_outs = [shape((rows, width), BF)] * PARTS
    gain = enc_gain.reshape(1, width)
    dma = pltpu.SemaphoreType.DMA

    up = group_blocks(enc_up, "x")
    down = group_blocks(enc_down.T, "zl")
    pair_own = jnp.concatenate([w_key, w_value], axis=1).T
    text_own = jnp.concatenate([w_query.T, w_out], axis=0)
    heads = group_blocks(jnp.concatenate([pair_own, text_own], axis=1), "x")

    text_normed = layer_norm(text_in, query_gain)[0].astype(BF)
    both = jnp.stack([text_normed, cotangent], axis=1)
    group_rows = []
    for other in range(4):
        block = lax.dynamic_index_in_dim(both, group ^ other, axis=0, keepdims=False)
        if other:
            block = lax.ppermute(block, ("yh", "core"), [(i, i ^ other) for i in range(4)])
        group_rows.append(block)
    caption = jnp.concatenate(group_rows, axis=1)
    caption = lax.all_gather(caption, "tensor", axis=0)

    act, slope, in_rows = pl.pallas_call(
        up_kernel,
        name="encoder_up",
        out_shape=[shape((patches, hidden), BF), shape((patches, hidden), F32), row_outs[0]],
        in_specs=[SMEM, ANY, VMEM] + [ANY] * 4,
        out_specs=[VMEM] * 3,
        scratch_shapes=[
            pltpu.VMEM((width, hidden), BF),
            pltpu.VMEM((patches, width), BF),
            dma((4,)),
            dma((PARTS,)),
        ],
        compiler_params=PARAMS,
    )(place, flat_in, gain, *up)
    branch = pl.pallas_call(
        down_kernel,
        name="encoder_down",
        out_shape=row_outs,
        in_specs=[SMEM, VMEM] + [ANY] * 4,
        out_specs=[VMEM] * PARTS,
        scratch_shapes=[pltpu.VMEM((width, hidden), BF), dma((4,))],
        compiler_params=PARAMS,
    )(place, act, *down)
    encoded_rows = (in_rows.astype(F32) + sum_blocks(branch)).astype(BF)
    encoded_blocks = gather_blocks(encoded_rows)

    head_shape = shape((4, PARTS * caption.shape[2], HEAD_DIM), BF)
    query, d_attn = pl.pallas_call(
        query_kernel,
        name="query",
        out_shape=[head_shape, head_shape],
        in_specs=[VMEM] + [ANY] * 4,
        out_specs=[VMEM] * 2,
        scratch_shapes=[pltpu.VMEM((4, 2 * HEAD_DIM, dec), BF), dma((4,))],
        compiler_params=PARAMS,
    )(caption, *heads)
    *term, encoded, d_pair = pl.pallas_call(
        attention_kernel,
        name="attention",
        out_shape=row_outs + [shape((patches, width), BF), shape((patches, 8 * HEAD_DIM), BF)],
        in_specs=[VMEM] * 6 + [ANY] * 4,
        out_specs=[VMEM] * 6,
        scratch_shapes=[pltpu.VMEM((4, 2 * HEAD_DIM, width), BF), dma((4,))],
        compiler_params=PARAMS,
    )(*encoded_blocks, query, d_attn, *heads)
    grad_rows = sum_blocks(term).astype(BF)
    grad_blocks = gather_blocks(grad_rows)

    pair_cols = 2 * HEAD_DIM
    cols = [d_pair[:, k * pair_cols : (k + 1) * pair_cols] for k in range(4)]
    contract = (((0,), (0,)), ((), ()))
    give = lax.dot_general(
        encoded, jnp.concatenate([cols[1], cols[3]], axis=1), contract, preferred_element_type=F32
    ).astype(BF)
    keep = lax.dot_general(
        encoded, jnp.concatenate([cols[0], cols[2]], axis=1), contract, preferred_element_type=F32
    )
    sums = (keep + swap(give, "core").astype(F32)).astype(BF)
    sums = scatter_sum(after(sums, grad_rows), "x")
    sums = sums[:, :pair_cols] + swap(sums[:, pair_cols:].astype(BF), "yh").astype(F32)
    sums = sums.reshape(8, -1, pair_cols)
    sums = halved(sums, "zh", 1)
    for bit in (2, 1):
        sums = halved(sums, "zl", bit)
    sums = sums[0]
    key_grad, value_grad = sums[:, :HEAD_DIM], sums[:, HEAD_DIM:]

    d_norm = pl.pallas_call(
        back_kernel,
        name="encoder_back",
        out_shape=row_outs,
        in_specs=[SMEM] + [VMEM] * 5 + [ANY] * 8,
        out_specs=[VMEM] * PARTS,
        scratch_shapes=[
            pltpu.VMEM((width, hidden), BF),
            pltpu.VMEM((width, hidden), BF),
            pltpu.VMEM((patches, width), BF),
            pltpu.VMEM((patches, hidden), BF),
            dma((4,)),
            dma((4,)),
        ],
        compiler_params=PARAMS,
    )(place, *grad_blocks, slope, *down, *up)
    d_normed = sum_blocks(d_norm)
    _, normal, inverse = layer_norm(in_rows, enc_gain)
    scaled_grad = d_normed * enc_gain
    d_input = inverse * (
        scaled_grad
        - jnp.mean(scaled_grad, axis=-1, keepdims=True)
        - normal * jnp.mean(scaled_grad * normal, axis=-1, keepdims=True)
    )
    image_rows = (grad_rows.astype(F32) + d_input).astype(BF)
    image_grad = lax.all_gather(image_rows, "tensor", axis=0, tiled=True).reshape(1, patches, width)
    return (image_grad, key_grad, value_grad)


def solution(mesh):
    fine = Mesh(
        mesh.devices.reshape(4, 2, 4, 4, 2, 2), ("x", "zh", "zl", "tensor", "yh", "core")
    )
    dp, group, heads = ("x", "zh", "zl"), ("yh", "core"), ("tensor", "yh", "core")
    in_specs = (
        P(dp + group, None, None),
        P(),
        P(group, "tensor"),
        P("tensor", group),
        P(dp, heads, None),
        P(),
        P(None, heads),
        P(None, heads),
        P(None, heads),
        P(heads, None),
        P(dp, heads, None),
    )
    out_specs = (P(dp + group, None, None), P(dp, heads), P(dp, heads))
    return jax.shard_map(local, mesh=fine, in_specs=in_specs, out_specs=out_specs, check_vma=False)
```

```python
import functools

import jax
import jax.numpy as jnp
from jax import lax
from jax.experimental import pallas as pl
from jax.experimental.pallas import tpu as pltpu
from jax.sharding import Mesh, PartitionSpec as P

HEAD_DIM = 128
EPSILON = 1e-06
BF = jnp.bfloat16
F32 = jnp.float32
PARTS = 4
COPIES = 2 + 2 * PARTS
PARAMS = pltpu.CompilerParams(vmem_limit_bytes=48 * 1024 * 1024)
VMEM = pl.BlockSpec(memory_space=pltpu.VMEM)
ANY = pl.BlockSpec(memory_space=pl.ANY)
SMEM = pl.BlockSpec(memory_space=pltpu.SMEM)
LAST = (((1,), (1,)), ((), ()))


def layer_norm(values, gain):
    floats = values.astype(F32)
    centre = jnp.mean(floats, axis=-1, keepdims=True)
    spread = jnp.mean(jnp.square(floats - centre), axis=-1, keepdims=True)
    inverse = lax.rsqrt(spread + EPSILON)
    normal = (floats - centre) * inverse
    return (normal * gain, normal, inverse)


def gelu_pair(values):
    c = 0.7978845608028654
    square = values * values
    tanh = jnp.tanh(c * values * (1.0 + 0.044715 * square))
    half = 0.5 * (1.0 + tanh)
    slope = half + 0.5 * values * (1.0 - tanh * tanh) * c * (1.0 + 3 * 0.044715 * square)
    return values * half, slope


def dot(a, b):
    return jnp.dot(a, b, preferred_element_type=F32)


def dot_last(a, b):
    return lax.dot_general(a, b, LAST, preferred_element_type=F32)


def block_copies(place, first, blocks, whole, sems):
    rows, cols = blocks[0].shape[0] // 2, blocks[0].shape[1]
    group = place[0]
    copies = []
    for bits, block in enumerate(blocks):
        source = block.at[pl.ds(first * rows, rows)]
        place_rows = pl.ds(pl.multiple_of((group ^ bits) * rows, 16), rows)
        if bits < 2:
            copies.append(pltpu.make_async_copy(source, whole.at[place_rows], sems.at[bits]))
            continue
        quarter = cols // PARTS
        for k in range(PARTS):
            start = pl.multiple_of(lax.rem(place[2] + k, PARTS) * quarter, 256)
            copies.append(
                pltpu.make_async_copy(
                    block.at[pl.ds(first * rows, rows), pl.ds(k * quarter, quarter)],
                    whole.at[place_rows, pl.ds(start, quarter)],
                    sems.at[PARTS * bits + k - 6],
                )
            )
    return copies


def up_kernel(
    place, image, gain, w0, w1, w2, w3, act, slope, in_rows, up, rows4, sems, row_sems
):
    weights = (w0, w1, w2, w3)
    copies = block_copies(place, 0, weights, up, sems)
    rows = in_rows.shape[0]
    moves = []
    for k in range(PARTS):
        start = pl.multiple_of(lax.rem(place[1] + PARTS - k, PARTS) * rows, 16)
        moves.append(
            pltpu.make_async_copy(
                image.at[pl.ds(start, rows)], rows4.at[pl.ds(k * rows, rows)], row_sems.at[k]
            )
        )
    for copy in moves + copies:
        copy.start()
    for copy in moves:
        copy.wait()
    in_rows[...] = rows4[pl.ds(0, rows)]
    normed = layer_norm(rows4[...], gain[...])[0].astype(BF)
    for copy in copies:
        copy.wait()
    for n in range(4):
        cols = pl.ds(n * 256, 256)
        value, grad = gelu_pair(dot(normed, up[:, cols]))
        act[:, cols] = value.astype(BF)
        slope[:, cols] = grad


def down_kernel(place, act, w0, w1, w2, w3, o0, o1, o2, o3, down, sems):
    weights = (w0, w1, w2, w3)
    copies = block_copies(place, 1, weights, down, sems)
    for copy in copies:
        copy.start()
    for copy in copies:
        copy.wait()
    split_rows(dot_last(act[...], down[...]).astype(BF), (o0, o1, o2, o3))


def split_rows(value, outs):
    rows = outs[0].shape[0]
    for k, out in enumerate(outs):
        out[...] = value[k * rows : (k + 1) * rows]


def query_kernel(c0, c1, c2, c3, p0, p1, p2, p3, query, d_attn, w, sems):
    captions = (c0, c1, c2, c3)
    dec = c0.shape[-1]
    skip = p0.shape[1] - dec
    copies = [
        pltpu.make_async_copy(p.at[:, pl.ds(skip, dec)], w.at[k], sems.at[k])
        for k, p in enumerate((p0, p1, p2, p3))
    ]
    for copy in copies:
        copy.start()
    text = jnp.concatenate([c[0] for c in captions], axis=0)
    cot = jnp.concatenate([c[1] for c in captions], axis=0)
    for k, copy in enumerate(copies):
        copy.wait()
        query[k] = (dot_last(text, w[k, :HEAD_DIM]) * HEAD_DIM ** (-0.5)).astype(BF)
        d_attn[k] = dot_last(cot, w[k, HEAD_DIM:]).astype(BF)


def attention_kernel(
    e0, e1, e2, e3, query, d_attn, p0, p1, p2, p3, o0, o1, o2, o3, encoded, d_pair, w, sems
):
    width = e0.shape[1]
    copies = [
        pltpu.make_async_copy(p.at[:, pl.ds(0, width)], w.at[k], sems.at[k])
        for k, p in enumerate((p0, p1, p2, p3))
    ]
    for copy in copies:
        copy.start()
    rows = e0.shape[0]
    for k, e in enumerate((e0, e1, e2, e3)):
        encoded[pl.ds(k * rows, rows)] = e[...]
    tokens = encoded[...]
    term = None
    for k, copy in enumerate(copies):
        copy.wait()
        pair = dot_last(tokens, w[k]).astype(BF)
        keys, values = pair[:, :HEAD_DIM], pair[:, HEAD_DIM:]
        q, da = query[k], d_attn[k]
        scores = dot_last(keys, q)
        expo = jnp.exp(scores - jnp.max(scores, axis=0, keepdims=True))
        probs = expo / jnp.sum(expo, axis=0, keepdims=True)
        d_probs = dot_last(values, da)
        mean = jnp.sum(probs * d_probs, axis=0, keepdims=True)
        d_scores = (probs * (d_probs - mean)).astype(BF)
        d_keys = dot(d_scores, q).astype(BF)
        d_values = dot(probs.astype(BF), da).astype(BF)
        grads = jnp.concatenate([d_keys, d_values], axis=1)
        d_pair[:, pl.ds(k * 2 * HEAD_DIM, 2 * HEAD_DIM)] = grads
    for k in range(PARTS):
        part = dot(d_pair[:, pl.ds(k * 2 * HEAD_DIM, 2 * HEAD_DIM)], w[k])
        term = part if term is None else term + part
    split_rows(term.astype(BF), (o0, o1, o2, o3))


def back_kernel(
    place, g0, g1, g2, g3, slope, w0, w1, w2, w3,
    o0, o1, o2, o3, down, up, grads, d_pre, down_sems, up_sems,
):
    weights = (w0, w1, w2, w3)
    first = block_copies(place, 1, weights, down, down_sems)
    second = block_copies(place, 0, weights, up, up_sems)
    for copy in first + second:
        copy.start()
    rows = g0.shape[0]
    for k, g in enumerate((g0, g1, g2, g3)):
        grads[pl.ds(k * rows, rows)] = g[...]
    for copy in first:
        copy.wait()
    for n in range(4):
        cols = pl.ds(n * 256, 256)
        d_pre[:, cols] = (dot(grads[...], down[:, cols]) * slope[:, cols]).astype(BF)
    for copy in second:
        copy.wait()
    split_rows(dot_last(d_pre[...], up[...]).astype(BF), (o0, o1, o2, o3))


def shift(value, axis, by):
    size = lax.axis_size(axis)
    return lax.ppermute(value, axis, [(i, (i + by) % size) for i in range(size)])


def swap(value, axis, bit=1):
    size = lax.axis_size(axis)
    return lax.ppermute(value, axis, [(i, i ^ bit) for i in range(size)])


def rows_at(value, start, size):
    return lax.dynamic_slice_in_dim(value, start, size, axis=0)


def after(value, *others):
    return lax.optimization_barrier((value,) + others)[0]


def quarter_of(value, which, dim):
    quarter = value.shape[dim] // PARTS
    return lax.dynamic_slice_in_dim(value, which * quarter, quarter, axis=dim)


def send_blocks(blocks):
    return [blocks[0]] + [shift(blocks[PARTS - by], "tensor", by) for by in range(1, PARTS)]


def add_blocks(blocks):
    total = blocks[0].astype(F32)
    for block in blocks[1:]:
        total = total + block.astype(F32)
    return total


def gather_blocks(block):
    return [block] + [shift(block, "tensor", by) for by in range(1, PARTS)]


def local(
    image_in, enc_gain, enc_up, enc_down, text_in, query_gain, w_query, w_key, w_value, w_out, cotangent
):
    _, patches, width = image_in.shape
    group = lax.axis_index("yh") * 2 + lax.axis_index("core")
    tensor = lax.axis_index("tensor")
    flat_in = image_in.reshape(patches, width)
    rows = patches // PARTS
    hidden = enc_up.shape[1]
    dec = w_query.shape[0]
    shape = jax.ShapeDtypeStruct
    row_outs = [shape((rows, width), BF)] * PARTS
    gain = enc_gain.reshape(1, width)
    dma = pltpu.SemaphoreType.DMA

    which = lax.rem(lax.axis_index("x") + lax.axis_index("zl"), PARTS)
    piece = jnp.concatenate(
        [quarter_of(enc_up, which, 1), quarter_of(enc_down, which, 0).T], axis=0
    )
    place = jnp.stack([group, tensor, which]).astype(jnp.int32)
    piece = swap(piece, "yh")
    pieces = [piece, shift(piece, "x", -1), shift(piece, "x", 2), shift(piece, ("zh", "zl"), 1)]
    far = jnp.concatenate(pieces, axis=1)
    own = jnp.concatenate([enc_up, enc_down.T], axis=0)
    weights = (own, swap(own, "core"), far, swap(far, "core"))
    pair_own = jnp.concatenate([w_key, w_value], axis=1).T
    text_own = jnp.concatenate([w_query.T, w_out], axis=0)
    heads_own = jnp.concatenate([pair_own, text_own], axis=1)

    heads_piece = swap(quarter_of(after(heads_own, piece), lax.axis_index("x"), 0), "yh")
    heads_near = swap(after(heads_own, far), "core")

    text_normed = layer_norm(text_in, query_gain)[0].astype(BF)
    both = after(jnp.stack([text_normed, cotangent], axis=1), far)
    both = both.reshape((2, 2) + both.shape[1:])
    core, yh = lax.axis_index("core"), lax.axis_index("yh")
    pick = functools.partial(lax.dynamic_index_in_dim, keepdims=False)
    near = jnp.concatenate([pick(both, core, 1), swap(pick(both, 1 - core, 1), "core")], axis=2)
    caption = jnp.concatenate([pick(near, yh, 0), swap(pick(near, 1 - yh, 0), "yh")], axis=1)

    act, slope, in_rows = pl.pallas_call(
        up_kernel,
        name="encoder_up",
        out_shape=[shape((patches, hidden), BF), shape((patches, hidden), F32), row_outs[0]],
        in_specs=[SMEM, ANY, VMEM] + [ANY] * 4,
        out_specs=[VMEM] * 3,
        scratch_shapes=[
            pltpu.VMEM((width, hidden), BF),
            pltpu.VMEM((patches, width), BF),
            dma((COPIES,)),
            dma((PARTS,)),
        ],
        compiler_params=PARAMS,
    )(place, flat_in, gain, *weights)
    branch = pl.pallas_call(
        down_kernel,
        name="encoder_down",
        out_shape=row_outs,
        in_specs=[SMEM, VMEM] + [ANY] * 4,
        out_specs=[VMEM] * PARTS,
        scratch_shapes=[pltpu.VMEM((width, hidden), BF), dma((COPIES,))],
        compiler_params=PARAMS,
    )(place, act, *weights)
    captions = gather_blocks(caption)
    *branch, c0, c1, c2, c3 = lax.optimization_barrier((*branch, *captions))
    captions = (c0, c1, c2, c3)
    encoded_rows = (in_rows.astype(F32) + add_blocks(send_blocks(branch))).astype(BF)
    encoded_blocks = gather_blocks(encoded_rows)

    heads_far = lax.all_gather(after(heads_piece, far), "x", axis=0, tiled=True)
    heads = (heads_own, heads_near, heads_far, swap(after(heads_far, encoded_rows), "core"))

    head_shape = shape((4, PARTS * caption.shape[1], HEAD_DIM), BF)
    query, d_attn = pl.pallas_call(
        query_kernel,
        name="query",
        out_shape=[head_shape, head_shape],
        in_specs=[VMEM] * PARTS + [ANY] * 4,
        out_specs=[VMEM] * 2,
        scratch_shapes=[pltpu.VMEM((4, 2 * HEAD_DIM, dec), BF), dma((4,))],
        compiler_params=PARAMS,
    )(*captions, *heads)
    *term, encoded, d_pair = pl.pallas_call(
        attention_kernel,
        name="attention",
        out_shape=row_outs + [shape((patches, width), BF), shape((patches, 8 * HEAD_DIM), BF)],
        in_specs=[VMEM] * 6 + [ANY] * 4,
        out_specs=[VMEM] * 6,
        scratch_shapes=[pltpu.VMEM((4, 2 * HEAD_DIM, width), BF), dma((4,))],
        compiler_params=PARAMS,
    )(*encoded_blocks, query, d_attn, *heads)
    term_blocks = send_blocks(term)
    grad_rows = add_blocks(term_blocks).astype(BF)
    grad_blocks = gather_blocks(grad_rows)

    pair_cols = 2 * HEAD_DIM
    cols = [d_pair[:, k * pair_cols : (k + 1) * pair_cols] for k in range(4)]
    contract = (((0,), (0,)), ((), ()))
    give = lax.dot_general(
        encoded, jnp.concatenate([cols[1], cols[3]], axis=1), contract, preferred_element_type=F32
    ).astype(BF)
    keep = lax.dot_general(
        encoded, jnp.concatenate([cols[0], cols[2]], axis=1), contract, preferred_element_type=F32
    )
    sums = (keep + swap(give, "core").astype(F32)).astype(BF)
    sums = lax.psum_scatter(sums, "x", scatter_dimension=0, tiled=True)
    sums = sums[:, :pair_cols].astype(F32) + swap(sums[:, pair_cols:], "yh").astype(F32)

    d_norm = pl.pallas_call(
        back_kernel,
        name="encoder_back",
        out_shape=row_outs,
        in_specs=[SMEM] + [VMEM] * 5 + [ANY] * 4,
        out_specs=[VMEM] * PARTS,
        scratch_shapes=[
            pltpu.VMEM((width, hidden), BF),
            pltpu.VMEM((width, hidden), BF),
            pltpu.VMEM((patches, width), BF),
            pltpu.VMEM((patches, hidden), BF),
            dma((COPIES,)),
            dma((COPIES,)),
        ],
        compiler_params=PARAMS,
    )(place, *grad_blocks, slope, *weights)
    *d_norm, sums = lax.optimization_barrier((*d_norm, sums))
    sums = sums.astype(BF).reshape(8, -1, pair_cols)
    sums = lax.all_to_all(sums, ("zh", "zl"), 0, 0, tiled=True)
    d_normed = add_blocks(send_blocks(d_norm))
    _, normal, inverse = layer_norm(in_rows, enc_gain)
    scaled_grad = d_normed * enc_gain
    d_input = inverse * (
        scaled_grad
        - jnp.mean(scaled_grad, axis=-1, keepdims=True)
        - normal * jnp.mean(scaled_grad * normal, axis=-1, keepdims=True)
    )
    image_rows = (grad_rows.astype(F32) + d_input).astype(BF)
    image_rows, sums = lax.optimization_barrier((image_rows, sums))
    sums = jnp.sum(sums.astype(F32), axis=0)
    key_grad, value_grad = sums[:, :HEAD_DIM], sums[:, HEAD_DIM:]
    image_grad = lax.all_gather(image_rows, "tensor", axis=0, tiled=True).reshape(1, patches, width)
    return (image_grad, key_grad, value_grad)


def solution(mesh):
    fine = Mesh(
        mesh.devices.reshape(4, 2, 4, 4, 2, 2), ("x", "zh", "zl", "tensor", "yh", "core")
    )
    dp, group, heads = ("x", "zh", "zl"), ("yh", "core"), ("tensor", "yh", "core")
    in_specs = (
        P(dp + group, None, None),
        P(),
        P(group, "tensor"),
        P("tensor", group),
        P(dp, heads, None),
        P(),
        P(None, heads),
        P(None, heads),
        P(None, heads),
        P(heads, None),
        P(dp, heads, None),
    )
    out_specs = (P(dp + group, None, None), P(dp, heads), P(dp, heads))
    return jax.shard_map(local, mesh=fine, in_specs=in_specs, out_specs=out_specs, check_vma=False)
```

```python
import functools

import jax
import jax.numpy as jnp
from jax import lax
from jax.experimental import pallas as pl
from jax.experimental.pallas import tpu as pltpu
from jax.sharding import Mesh, PartitionSpec as P

HEAD_DIM = 128
EPSILON = 1e-06
BF = jnp.bfloat16
F32 = jnp.float32
PARTS = 4
COPIES = 2 + 2 * PARTS
PARAMS = pltpu.CompilerParams(vmem_limit_bytes=48 * 1024 * 1024)
VMEM = pl.BlockSpec(memory_space=pltpu.VMEM)
ANY = pl.BlockSpec(memory_space=pl.ANY)
SMEM = pl.BlockSpec(memory_space=pltpu.SMEM)
LAST = (((1,), (1,)), ((), ()))


def layer_norm(values, gain):
    floats = values.astype(F32)
    centre = jnp.mean(floats, axis=-1, keepdims=True)
    spread = jnp.mean(jnp.square(floats - centre), axis=-1, keepdims=True)
    inverse = lax.rsqrt(spread + EPSILON)
    normal = (floats - centre) * inverse
    return (normal * gain, normal, inverse)


def gelu_pair(values):
    c = 0.7978845608028654
    square = values * values
    tanh = jnp.tanh(c * values * (1.0 + 0.044715 * square))
    half = 0.5 * (1.0 + tanh)
    slope = half + 0.5 * values * (1.0 - tanh * tanh) * c * (1.0 + 3 * 0.044715 * square)
    return values * half, slope


def dot(a, b):
    return jnp.dot(a, b, preferred_element_type=F32)


def dot_last(a, b):
    return lax.dot_general(a, b, LAST, preferred_element_type=F32)


def block_copies(place, first, blocks, whole, sems):
    rows, cols = blocks[0].shape[0] // 2, blocks[0].shape[1]
    group = place[0]
    copies = []
    for bits, block in enumerate(blocks):
        source = block.at[pl.ds(first * rows, rows)]
        place_rows = pl.ds(pl.multiple_of((group ^ bits) * rows, 16), rows)
        if bits < 2:
            copies.append(pltpu.make_async_copy(source, whole.at[place_rows], sems.at[bits]))
            continue
        quarter = cols // PARTS
        for k in range(PARTS):
            start = pl.multiple_of(lax.rem(place[2] + k, PARTS) * quarter, 256)
            copies.append(
                pltpu.make_async_copy(
                    block.at[pl.ds(first * rows, rows), pl.ds(k * quarter, quarter)],
                    whole.at[place_rows, pl.ds(start, quarter)],
                    sems.at[PARTS * bits + k - 6],
                )
            )
    return copies


def up_kernel(
    place, image, gain, w0, w1, w2, w3, act, slope, in_rows, up, rows4, sems, row_sems
):
    weights = (w0, w1, w2, w3)
    copies = block_copies(place, 0, weights, up, sems)
    rows = in_rows.shape[0]
    moves = []
    for k in range(PARTS):
        start = pl.multiple_of(lax.rem(place[1] + PARTS - k, PARTS) * rows, 16)
        moves.append(
            pltpu.make_async_copy(
                image.at[pl.ds(start, rows)], rows4.at[pl.ds(k * rows, rows)], row_sems.at[k]
            )
        )
    for copy in moves + copies:
        copy.start()
    for copy in moves:
        copy.wait()
    in_rows[...] = rows4[pl.ds(0, rows)]
    normed = layer_norm(rows4[...], gain[...])[0].astype(BF)
    for copy in copies:
        copy.wait()
    for n in range(4):
        cols = pl.ds(n * 256, 256)
        value, grad = gelu_pair(dot(normed, up[:, cols]))
        act[:, cols] = value.astype(BF)
        slope[:, cols] = grad


def down_kernel(place, act, w0, w1, w2, w3, o0, o1, o2, o3, down, sems):
    weights = (w0, w1, w2, w3)
    copies = block_copies(place, 1, weights, down, sems)
    for copy in copies:
        copy.start()
    for copy in copies:
        copy.wait()
    split_rows(dot_last(act[...], down[...]).astype(BF), (o0, o1, o2, o3))


def split_rows(value, outs):
    rows = outs[0].shape[0]
    for k, out in enumerate(outs):
        out[...] = value[k * rows : (k + 1) * rows]


def query_kernel(caption, p0, p1, p2, p3, query, d_attn, w, sems):
    dec = caption.shape[-1]
    skip = p0.shape[1] - dec
    copies = [
        pltpu.make_async_copy(p.at[:, pl.ds(skip, dec)], w.at[k], sems.at[k])
        for k, p in enumerate((p0, p1, p2, p3))
    ]
    for copy in copies:
        copy.start()
    text, cot = caption[0], caption[1]
    for k, copy in enumerate(copies):
        copy.wait()
        query[k] = (dot_last(text, w[k, :HEAD_DIM]) * HEAD_DIM ** (-0.5)).astype(BF)
        d_attn[k] = dot_last(cot, w[k, HEAD_DIM:]).astype(BF)


def attention_kernel(
    e0, e1, e2, e3, query, d_attn, p0, p1, p2, p3, o0, o1, o2, o3, encoded, d_pair, w, sems
):
    width = e0.shape[1]
    copies = [
        pltpu.make_async_copy(p.at[:, pl.ds(0, width)], w.at[k], sems.at[k])
        for k, p in enumerate((p0, p1, p2, p3))
    ]
    for copy in copies:
        copy.start()
    rows = e0.shape[0]
    for k, e in enumerate((e0, e1, e2, e3)):
        encoded[pl.ds(k * rows, rows)] = e[...]
    tokens = encoded[...]
    term = None
    for k, copy in enumerate(copies):
        copy.wait()
        pair = dot_last(tokens, w[k]).astype(BF)
        keys, values = pair[:, :HEAD_DIM], pair[:, HEAD_DIM:]
        q, da = query[k], d_attn[k]
        scores = dot_last(keys, q)
        expo = jnp.exp(scores - jnp.max(scores, axis=0, keepdims=True))
        probs = expo / jnp.sum(expo, axis=0, keepdims=True)
        d_probs = dot_last(values, da)
        mean = jnp.sum(probs * d_probs, axis=0, keepdims=True)
        d_scores = (probs * (d_probs - mean)).astype(BF)
        d_keys = dot(d_scores, q).astype(BF)
        d_values = dot(probs.astype(BF), da).astype(BF)
        grads = jnp.concatenate([d_keys, d_values], axis=1)
        d_pair[:, pl.ds(k * 2 * HEAD_DIM, 2 * HEAD_DIM)] = grads
    for k in range(PARTS):
        part = dot(d_pair[:, pl.ds(k * 2 * HEAD_DIM, 2 * HEAD_DIM)], w[k])
        term = part if term is None else term + part
    split_rows(term.astype(BF), (o0, o1, o2, o3))


def back_kernel(
    place, g0, g1, g2, g3, slope, w0, w1, w2, w3,
    o0, o1, o2, o3, down, up, grads, d_pre, down_sems, up_sems,
):
    weights = (w0, w1, w2, w3)
    first = block_copies(place, 1, weights, down, down_sems)
    second = block_copies(place, 0, weights, up, up_sems)
    for copy in first + second:
        copy.start()
    rows = g0.shape[0]
    for k, g in enumerate((g0, g1, g2, g3)):
        grads[pl.ds(k * rows, rows)] = g[...]
    for copy in first:
        copy.wait()
    for n in range(4):
        cols = pl.ds(n * 256, 256)
        d_pre[:, cols] = (dot(grads[...], down[:, cols]) * slope[:, cols]).astype(BF)
    for copy in second:
        copy.wait()
    split_rows(dot_last(d_pre[...], up[...]).astype(BF), (o0, o1, o2, o3))


def shift(value, axis, by):
    size = lax.axis_size(axis)
    return lax.ppermute(value, axis, [(i, (i + by) % size) for i in range(size)])


def swap(value, axis, bit=1):
    size = lax.axis_size(axis)
    return lax.ppermute(value, axis, [(i, i ^ bit) for i in range(size)])


def rows_at(value, start, size):
    return lax.dynamic_slice_in_dim(value, start, size, axis=0)


def after(value, *others):
    return lax.optimization_barrier((value,) + others)[0]


def quarter_of(value, which, dim):
    quarter = value.shape[dim] // PARTS
    return lax.dynamic_slice_in_dim(value, which * quarter, quarter, axis=dim)


def send_blocks(blocks):
    return [blocks[0]] + [shift(blocks[PARTS - by], "tensor", by) for by in range(1, PARTS)]


def add_blocks(blocks):
    total = blocks[0].astype(F32)
    for block in blocks[1:]:
        total = total + block.astype(F32)
    return total


def gather_blocks(block):
    return [block] + [shift(block, "tensor", by) for by in range(1, PARTS)]


def local(
    image_in, enc_gain, enc_up, enc_down, text_in, query_gain, w_query, w_key, w_value, w_out, cotangent
):
    _, patches, width = image_in.shape
    group = lax.axis_index("yh") * 2 + lax.axis_index("core")
    tensor = lax.axis_index("tensor")
    flat_in = image_in.reshape(patches, width)
    rows = patches // PARTS
    hidden = enc_up.shape[1]
    dec = w_query.shape[0]
    shape = jax.ShapeDtypeStruct
    row_outs = [shape((rows, width), BF)] * PARTS
    gain = enc_gain.reshape(1, width)
    dma = pltpu.SemaphoreType.DMA

    which = lax.rem(lax.axis_index("x") + lax.axis_index("zl"), PARTS)
    piece = jnp.concatenate(
        [quarter_of(enc_up, which, 1), quarter_of(enc_down, which, 0).T], axis=0
    )
    place = jnp.stack([group, tensor, which]).astype(jnp.int32)
    piece = swap(piece, "yh")
    pieces = [piece, shift(piece, "x", -1), shift(piece, "x", 2), shift(piece, ("zh", "zl"), 1)]
    far = jnp.concatenate(pieces, axis=1)
    own = jnp.concatenate([enc_up, enc_down.T], axis=0)
    weights = (own, swap(own, "core"), far, swap(far, "core"))
    pair_own = jnp.concatenate([w_key, w_value], axis=1).T
    text_own = jnp.concatenate([w_query.T, w_out], axis=0)
    heads_own = jnp.concatenate([pair_own, text_own], axis=1)

    heads_piece = swap(quarter_of(after(heads_own, piece), lax.axis_index("x"), 0), "yh")
    heads_near = swap(after(heads_own, far), "core")

    text_normed = layer_norm(text_in, query_gain)[0].astype(BF)
    both = after(jnp.stack([text_normed, cotangent], axis=1), piece)
    sent = jnp.broadcast_to(both, (PARTS,) + both.shape).reshape((-1,) + both.shape[1:])
    caption = lax.all_to_all(sent, ("tensor", "yh", "core"), 0, 0, tiled=True)

    act, slope, in_rows = pl.pallas_call(
        up_kernel,
        name="encoder_up",
        out_shape=[shape((patches, hidden), BF), shape((patches, hidden), F32), row_outs[0]],
        in_specs=[SMEM, ANY, VMEM] + [ANY] * 4,
        out_specs=[VMEM] * 3,
        scratch_shapes=[
            pltpu.VMEM((width, hidden), BF),
            pltpu.VMEM((patches, width), BF),
            dma((COPIES,)),
            dma((PARTS,)),
        ],
        compiler_params=PARAMS,
    )(place, flat_in, gain, *weights)
    branch = pl.pallas_call(
        down_kernel,
        name="encoder_down",
        out_shape=row_outs,
        in_specs=[SMEM, VMEM] + [ANY] * 4,
        out_specs=[VMEM] * PARTS,
        scratch_shapes=[pltpu.VMEM((width, hidden), BF), dma((COPIES,))],
        compiler_params=PARAMS,
    )(place, act, *weights)
    *branch, caption = lax.optimization_barrier((*branch, caption))
    caption = jnp.swapaxes(caption, 0, 1).reshape(2, -1, dec)
    encoded_rows = (in_rows.astype(F32) + add_blocks(send_blocks(branch))).astype(BF)
    encoded_blocks = gather_blocks(encoded_rows)

    heads_far = lax.all_gather(after(heads_piece, far), "x", axis=0, tiled=True)
    heads = (heads_own, heads_near, heads_far, swap(after(heads_far, encoded_rows), "core"))

    head_shape = shape((4, caption.shape[1], HEAD_DIM), BF)
    query, d_attn = pl.pallas_call(
        query_kernel,
        name="query",
        out_shape=[head_shape, head_shape],
        in_specs=[VMEM] + [ANY] * 4,
        out_specs=[VMEM] * 2,
        scratch_shapes=[pltpu.VMEM((4, 2 * HEAD_DIM, dec), BF), dma((4,))],
        compiler_params=PARAMS,
    )(caption, *heads)
    *term, encoded, d_pair = pl.pallas_call(
        attention_kernel,
        name="attention",
        out_shape=row_outs + [shape((patches, width), BF), shape((patches, 8 * HEAD_DIM), BF)],
        in_specs=[VMEM] * 6 + [ANY] * 4,
        out_specs=[VMEM] * 6,
        scratch_shapes=[pltpu.VMEM((4, 2 * HEAD_DIM, width), BF), dma((4,))],
        compiler_params=PARAMS,
    )(*encoded_blocks, query, d_attn, *heads)
    term_blocks = send_blocks(term)
    grad_rows = add_blocks(term_blocks).astype(BF)
    grad_blocks = gather_blocks(grad_rows)

    pair_cols = 2 * HEAD_DIM
    cols = [d_pair[:, k * pair_cols : (k + 1) * pair_cols] for k in range(4)]
    contract = (((0,), (0,)), ((), ()))
    give = lax.dot_general(
        encoded, jnp.concatenate([cols[1], cols[3]], axis=1), contract, preferred_element_type=F32
    ).astype(BF)
    keep = lax.dot_general(
        encoded, jnp.concatenate([cols[0], cols[2]], axis=1), contract, preferred_element_type=F32
    )
    sums = (keep + swap(give, "core").astype(F32)).astype(BF)
    sums = lax.psum_scatter(sums, "x", scatter_dimension=0, tiled=True)
    sums = sums[:, :pair_cols].astype(F32) + swap(sums[:, pair_cols:], "yh").astype(F32)

    d_norm = pl.pallas_call(
        back_kernel,
        name="encoder_back",
        out_shape=row_outs,
        in_specs=[SMEM] + [VMEM] * 5 + [ANY] * 4,
        out_specs=[VMEM] * PARTS,
        scratch_shapes=[
            pltpu.VMEM((width, hidden), BF),
            pltpu.VMEM((width, hidden), BF),
            pltpu.VMEM((patches, width), BF),
            pltpu.VMEM((patches, hidden), BF),
            dma((COPIES,)),
            dma((COPIES,)),
        ],
        compiler_params=PARAMS,
    )(place, *grad_blocks, slope, *weights)
    *d_norm, sums = lax.optimization_barrier((*d_norm, sums))
    sums = sums.astype(BF).reshape(8, -1, pair_cols)
    sums = lax.all_to_all(sums, ("zh", "zl"), 0, 0, tiled=True)
    d_normed = add_blocks(send_blocks(d_norm))
    _, normal, inverse = layer_norm(in_rows, enc_gain)
    scaled_grad = d_normed * enc_gain
    d_input = inverse * (
        scaled_grad
        - jnp.mean(scaled_grad, axis=-1, keepdims=True)
        - normal * jnp.mean(scaled_grad * normal, axis=-1, keepdims=True)
    )
    image_rows = (grad_rows.astype(F32) + d_input).astype(BF)
    image_rows, sums = lax.optimization_barrier((image_rows, sums))
    sums = jnp.sum(sums.astype(F32), axis=0)
    key_grad, value_grad = sums[:, :HEAD_DIM], sums[:, HEAD_DIM:]
    image_grad = lax.all_gather(image_rows, "tensor", axis=0, tiled=True).reshape(1, patches, width)
    return (image_grad, key_grad, value_grad)


def solution(mesh):
    fine = Mesh(
        mesh.devices.reshape(4, 2, 4, 4, 2, 2), ("x", "zh", "zl", "tensor", "yh", "core")
    )
    dp, group, heads = ("x", "zh", "zl"), ("yh", "core"), ("tensor", "yh", "core")
    in_specs = (
        P(dp + group, None, None),
        P(),
        P(group, "tensor"),
        P("tensor", group),
        P(dp, heads, None),
        P(),
        P(None, heads),
        P(None, heads),
        P(None, heads),
        P(heads, None),
        P(dp, heads, None),
    )
    out_specs = (P(dp + group, None, None), P(dp, heads), P(dp, heads))
    return jax.shard_map(local, mesh=fine, in_specs=in_specs, out_specs=out_specs, check_vma=False)
```

```python
import functools

import jax
import jax.numpy as jnp
from jax import lax
from jax.experimental import pallas as pl
from jax.experimental.pallas import tpu as pltpu
from jax.sharding import Mesh, PartitionSpec as P

HEAD_DIM = 128
EPSILON = 1e-06
BF = jnp.bfloat16
F32 = jnp.float32
PARTS = 4
COPIES = 2 + 2 * PARTS
PARAMS = pltpu.CompilerParams(vmem_limit_bytes=48 * 1024 * 1024)
VMEM = pl.BlockSpec(memory_space=pltpu.VMEM)
ANY = pl.BlockSpec(memory_space=pl.ANY)
SMEM = pl.BlockSpec(memory_space=pltpu.SMEM)
LAST = (((1,), (1,)), ((), ()))


def layer_norm(values, gain):
    floats = values.astype(F32)
    centre = jnp.mean(floats, axis=-1, keepdims=True)
    spread = jnp.mean(jnp.square(floats - centre), axis=-1, keepdims=True)
    inverse = lax.rsqrt(spread + EPSILON)
    normal = (floats - centre) * inverse
    return (normal * gain, normal, inverse)


def gelu_pair(values):
    c = 0.7978845608028654
    square = values * values
    tanh = jnp.tanh(c * values * (1.0 + 0.044715 * square))
    half = 0.5 * (1.0 + tanh)
    slope = half + 0.5 * values * (1.0 - tanh * tanh) * c * (1.0 + 3 * 0.044715 * square)
    return values * half, slope


def dot(a, b):
    return jnp.dot(a, b, preferred_element_type=F32)


def dot_last(a, b):
    return lax.dot_general(a, b, LAST, preferred_element_type=F32)


def block_copies(place, first, blocks, whole, sems):
    rows, cols = blocks[0].shape[0] // 2, blocks[0].shape[1]
    group = place[0]
    copies = []
    for bits, block in enumerate(blocks):
        source = block.at[pl.ds(first * rows, rows)]
        place_rows = pl.ds(pl.multiple_of((group ^ bits) * rows, 16), rows)
        if bits < 2:
            copies.append(pltpu.make_async_copy(source, whole.at[place_rows], sems.at[bits]))
            continue
        quarter = cols // PARTS
        for k in range(PARTS):
            start = pl.multiple_of(lax.rem(place[2] + k, PARTS) * quarter, 256)
            copies.append(
                pltpu.make_async_copy(
                    block.at[pl.ds(first * rows, rows), pl.ds(k * quarter, quarter)],
                    whole.at[place_rows, pl.ds(start, quarter)],
                    sems.at[PARTS * bits + k - 6],
                )
            )
    return copies


def up_kernel(
    place, image, gain, w0, w1, w2, w3, act, slope, in_rows, up, rows4, sems, row_sems
):
    weights = (w0, w1, w2, w3)
    copies = block_copies(place, 0, weights, up, sems)
    rows = in_rows.shape[0]
    moves = []
    for k in range(PARTS):
        start = pl.multiple_of(lax.rem(place[1] + PARTS - k, PARTS) * rows, 16)
        moves.append(
            pltpu.make_async_copy(
                image.at[pl.ds(start, rows)], rows4.at[pl.ds(k * rows, rows)], row_sems.at[k]
            )
        )
    for copy in moves + copies:
        copy.start()
    for copy in moves:
        copy.wait()
    in_rows[...] = rows4[pl.ds(0, rows)]
    normed = layer_norm(rows4[...], gain[...])[0].astype(BF)
    for copy in copies:
        copy.wait()
    for n in range(4):
        cols = pl.ds(n * 256, 256)
        value, grad = gelu_pair(dot(normed, up[:, cols]))
        act[:, cols] = value.astype(BF)
        slope[:, cols] = grad


def down_kernel(place, act, w0, w1, w2, w3, o0, o1, o2, o3, down, sems):
    weights = (w0, w1, w2, w3)
    copies = block_copies(place, 1, weights, down, sems)
    for copy in copies:
        copy.start()
    for copy in copies:
        copy.wait()
    split_rows(dot_last(act[...], down[...]).astype(BF), (o0, o1, o2, o3))


def split_rows(value, outs):
    rows = outs[0].shape[0]
    for k, out in enumerate(outs):
        out[...] = value[k * rows : (k + 1) * rows]


def query_kernel(caption, p0, p1, p2, p3, query, d_attn, w, sems):
    dec = caption.shape[-1]
    skip = p0.shape[1] - dec
    copies = [
        pltpu.make_async_copy(p.at[:, pl.ds(skip, dec)], w.at[k], sems.at[k])
        for k, p in enumerate((p0, p1, p2, p3))
    ]
    for copy in copies:
        copy.start()
    text, cot = caption[0], caption[1]
    for k, copy in enumerate(copies):
        copy.wait()
        query[k] = (dot_last(text, w[k, :HEAD_DIM]) * HEAD_DIM ** (-0.5)).astype(BF)
        d_attn[k] = dot_last(cot, w[k, HEAD_DIM:]).astype(BF)


def attention_kernel(
    e0, e1, e2, e3, query, d_attn, p0, p1, p2, p3, o0, o1, o2, o3, encoded, d_pair, w, sems
):
    width = e0.shape[1]
    copies = [
        pltpu.make_async_copy(p.at[:, pl.ds(0, width)], w.at[k], sems.at[k])
        for k, p in enumerate((p0, p1, p2, p3))
    ]
    for copy in copies:
        copy.start()
    rows = e0.shape[0]
    for k, e in enumerate((e0, e1, e2, e3)):
        encoded[pl.ds(k * rows, rows)] = e[...]
    tokens = encoded[...]
    term = None
    for k, copy in enumerate(copies):
        copy.wait()
        pair = dot_last(tokens, w[k]).astype(BF)
        keys, values = pair[:, :HEAD_DIM], pair[:, HEAD_DIM:]
        q, da = query[k], d_attn[k]
        scores = dot_last(keys, q)
        expo = jnp.exp(scores - jnp.max(scores, axis=0, keepdims=True))
        probs = expo / jnp.sum(expo, axis=0, keepdims=True)
        d_probs = dot_last(values, da)
        mean = jnp.sum(probs * d_probs, axis=0, keepdims=True)
        d_scores = (probs * (d_probs - mean)).astype(BF)
        d_keys = dot(d_scores, q).astype(BF)
        d_values = dot(probs.astype(BF), da).astype(BF)
        grads = jnp.concatenate([d_keys, d_values], axis=1)
        d_pair[:, pl.ds(k * 2 * HEAD_DIM, 2 * HEAD_DIM)] = grads
    for k in range(PARTS):
        part = dot(d_pair[:, pl.ds(k * 2 * HEAD_DIM, 2 * HEAD_DIM)], w[k])
        term = part if term is None else term + part
    split_rows(term.astype(BF), (o0, o1, o2, o3))


def back_kernel(
    place, g0, g1, g2, g3, slope, w0, w1, w2, w3,
    o0, o1, o2, o3, down, up, grads, d_pre, down_sems, up_sems,
):
    weights = (w0, w1, w2, w3)
    first = block_copies(place, 1, weights, down, down_sems)
    second = block_copies(place, 0, weights, up, up_sems)
    for copy in first + second:
        copy.start()
    rows = g0.shape[0]
    for k, g in enumerate((g0, g1, g2, g3)):
        grads[pl.ds(k * rows, rows)] = g[...]
    for copy in first:
        copy.wait()
    for n in range(4):
        cols = pl.ds(n * 256, 256)
        d_pre[:, cols] = (dot(grads[...], down[:, cols]) * slope[:, cols]).astype(BF)
    for copy in second:
        copy.wait()
    split_rows(dot_last(d_pre[...], up[...]).astype(BF), (o0, o1, o2, o3))


def shift(value, axis, by):
    size = lax.axis_size(axis)
    return lax.ppermute(value, axis, [(i, (i + by) % size) for i in range(size)])


def swap(value, axis, bit=1):
    size = lax.axis_size(axis)
    return lax.ppermute(value, axis, [(i, i ^ bit) for i in range(size)])


def rows_at(value, start, size):
    return lax.dynamic_slice_in_dim(value, start, size, axis=0)


def after(value, *others):
    return lax.optimization_barrier((value,) + others)[0]


def quarter_of(value, which, dim):
    quarter = value.shape[dim] // PARTS
    return lax.dynamic_slice_in_dim(value, which * quarter, quarter, axis=dim)


def send_blocks(blocks):
    return [blocks[0]] + [shift(blocks[PARTS - by], "tensor", by) for by in range(1, PARTS)]


def add_blocks(blocks):
    total = blocks[0].astype(F32)
    for block in blocks[1:]:
        total = total + block.astype(F32)
    return total


def gather_blocks(block):
    return [block] + [shift(block, "tensor", by) for by in range(1, PARTS)]


def local(
    image_in, enc_gain, enc_up, enc_down, text_in, query_gain, w_query, w_key, w_value, w_out, cotangent
):
    _, patches, width = image_in.shape
    group = lax.axis_index("yh") * 2 + lax.axis_index("core")
    tensor = lax.axis_index("tensor")
    flat_in = image_in.reshape(patches, width)
    rows = patches // PARTS
    hidden = enc_up.shape[1]
    dec = w_query.shape[0]
    shape = jax.ShapeDtypeStruct
    row_outs = [shape((rows, width), BF)] * PARTS
    gain = enc_gain.reshape(1, width)
    dma = pltpu.SemaphoreType.DMA

    which = lax.rem(lax.axis_index("x") + lax.axis_index("zl"), PARTS)
    piece = jnp.concatenate(
        [quarter_of(enc_up, which, 1), quarter_of(enc_down, which, 0).T], axis=0
    )
    place = jnp.stack([group, tensor, which]).astype(jnp.int32)
    piece = swap(piece, "yh")
    pieces = [piece, shift(piece, "x", -1), shift(piece, "x", 2), shift(piece, ("zh", "zl"), 1)]
    far = jnp.concatenate(pieces, axis=1)
    own = jnp.concatenate([enc_up, enc_down.T], axis=0)
    weights = (own, swap(own, "core"), far, swap(far, "core"))
    pair_own = jnp.concatenate([w_key, w_value], axis=1).T
    text_own = jnp.concatenate([w_query.T, w_out], axis=0)
    heads_own = jnp.concatenate([pair_own, text_own], axis=1)

    heads_piece = swap(quarter_of(after(heads_own, piece), lax.axis_index("x"), 0), "yh")
    heads_near = swap(after(heads_own, far), "core")

    text_normed = layer_norm(text_in, query_gain)[0].astype(BF)
    both = after(jnp.stack([text_normed, cotangent], axis=1), piece)
    sent = jnp.broadcast_to(both, (PARTS,) + both.shape).reshape((-1,) + both.shape[1:])
    caption = lax.all_to_all(sent, ("tensor", "yh", "core"), 0, 0, tiled=True)

    act, slope, in_rows = pl.pallas_call(
        up_kernel,
        name="encoder_up",
        out_shape=[shape((patches, hidden), BF), shape((patches, hidden), F32), row_outs[0]],
        in_specs=[SMEM, ANY, VMEM] + [ANY] * 4,
        out_specs=[VMEM] * 3,
        scratch_shapes=[
            pltpu.VMEM((width, hidden), BF),
            pltpu.VMEM((patches, width), BF),
            dma((COPIES,)),
            dma((PARTS,)),
        ],
        compiler_params=PARAMS,
    )(place, flat_in, gain, *weights)
    branch = pl.pallas_call(
        down_kernel,
        name="encoder_down",
        out_shape=row_outs,
        in_specs=[SMEM, VMEM] + [ANY] * 4,
        out_specs=[VMEM] * PARTS,
        scratch_shapes=[pltpu.VMEM((width, hidden), BF), dma((COPIES,))],
        compiler_params=PARAMS,
    )(place, act, *weights)
    branch = list(branch)
    branch[1], caption = lax.optimization_barrier((branch[1], caption))
    caption = jnp.swapaxes(caption, 0, 1).reshape(2, -1, dec)
    encoded_rows = (in_rows.astype(F32) + add_blocks(send_blocks(branch))).astype(BF)
    encoded_blocks = gather_blocks(encoded_rows)

    heads_far = lax.all_gather(after(heads_piece, far), "x", axis=0, tiled=True)
    heads = (heads_own, heads_near, heads_far, swap(after(heads_far, encoded_rows), "core"))

    head_shape = shape((4, caption.shape[1], HEAD_DIM), BF)
    query, d_attn = pl.pallas_call(
        query_kernel,
        name="query",
        out_shape=[head_shape, head_shape],
        in_specs=[VMEM] + [ANY] * 4,
        out_specs=[VMEM] * 2,
        scratch_shapes=[pltpu.VMEM((4, 2 * HEAD_DIM, dec), BF), dma((4,))],
        compiler_params=PARAMS,
    )(caption, *heads)
    *term, encoded, d_pair = pl.pallas_call(
        attention_kernel,
        name="attention",
        out_shape=row_outs + [shape((patches, width), BF), shape((patches, 8 * HEAD_DIM), BF)],
        in_specs=[VMEM] * 6 + [ANY] * 4,
        out_specs=[VMEM] * 6,
        scratch_shapes=[pltpu.VMEM((4, 2 * HEAD_DIM, width), BF), dma((4,))],
        compiler_params=PARAMS,
    )(*encoded_blocks, query, d_attn, *heads)
    term_blocks = send_blocks(term)
    grad_rows = add_blocks(term_blocks).astype(BF)
    grad_blocks = gather_blocks(grad_rows)

    pair_cols = 2 * HEAD_DIM
    cols = [d_pair[:, k * pair_cols : (k + 1) * pair_cols] for k in range(4)]
    contract = (((0,), (0,)), ((), ()))
    give = lax.dot_general(
        encoded, jnp.concatenate([cols[1], cols[3]], axis=1), contract, preferred_element_type=F32
    ).astype(BF)
    later = [after(cols[0], grad_rows), after(cols[2], grad_rows)]
    keep = lax.dot_general(
        encoded, jnp.concatenate(later, axis=1), contract, preferred_element_type=F32
    )
    sums = (keep + swap(give, "core").astype(F32)).astype(BF)
    sums = lax.psum_scatter(sums, "x", scatter_dimension=0, tiled=True)

    d_norm = pl.pallas_call(
        back_kernel,
        name="encoder_back",
        out_shape=row_outs,
        in_specs=[SMEM] + [VMEM] * 5 + [ANY] * 4,
        out_specs=[VMEM] * PARTS,
        scratch_shapes=[
            pltpu.VMEM((width, hidden), BF),
            pltpu.VMEM((width, hidden), BF),
            pltpu.VMEM((patches, width), BF),
            pltpu.VMEM((patches, hidden), BF),
            dma((COPIES,)),
            dma((COPIES,)),
        ],
        compiler_params=PARAMS,
    )(place, *grad_blocks, slope, *weights)
    d_norm = list(d_norm)
    d_norm[1], sums = lax.optimization_barrier((d_norm[1], sums))
    sums = lax.all_to_all(sums.reshape(8, -1, 2 * pair_cols), ("zh", "zl"), 0, 0, tiled=True)
    d_normed = add_blocks(send_blocks(d_norm))
    _, normal, inverse = layer_norm(in_rows, enc_gain)
    scaled_grad = d_normed * enc_gain
    d_input = inverse * (
        scaled_grad
        - jnp.mean(scaled_grad, axis=-1, keepdims=True)
        - normal * jnp.mean(scaled_grad * normal, axis=-1, keepdims=True)
    )
    image_rows = (grad_rows.astype(F32) + d_input).astype(BF)
    image_grad = lax.all_gather(image_rows, "tensor", axis=0, tiled=True).reshape(1, patches, width)
    image_grad, sums = lax.optimization_barrier((image_grad, sums))
    sums = jnp.sum(sums.astype(F32), axis=0)
    sums = sums[:, :pair_cols] + swap(sums[:, pair_cols:].astype(BF), "yh").astype(F32)
    key_grad, value_grad = sums[:, :HEAD_DIM], sums[:, HEAD_DIM:]
    return (image_grad, key_grad, value_grad)


def solution(mesh):
    fine = Mesh(
        mesh.devices.reshape(4, 2, 4, 4, 2, 2), ("x", "zh", "zl", "tensor", "yh", "core")
    )
    dp, group, heads = ("x", "zh", "zl"), ("yh", "core"), ("tensor", "yh", "core")
    in_specs = (
        P(dp + group, None, None),
        P(),
        P(group, "tensor"),
        P("tensor", group),
        P(dp, heads, None),
        P(),
        P(None, heads),
        P(None, heads),
        P(None, heads),
        P(heads, None),
        P(dp, heads, None),
    )
    out_specs = (P(dp + group, None, None), P(dp, heads), P(dp, heads))
    return jax.shard_map(local, mesh=fine, in_specs=in_specs, out_specs=out_specs, check_vma=False)
```

```python
import functools

import jax
import jax.numpy as jnp
from jax import lax
from jax.experimental import pallas as pl
from jax.experimental.pallas import tpu as pltpu
from jax.sharding import Mesh, PartitionSpec as P

HEAD_DIM = 128
EPSILON = 1e-06
BF = jnp.bfloat16
F32 = jnp.float32
PARTS = 4
COPIES = 2 + 2 * PARTS
PARAMS = pltpu.CompilerParams(vmem_limit_bytes=48 * 1024 * 1024)
VMEM = pl.BlockSpec(memory_space=pltpu.VMEM)
ANY = pl.BlockSpec(memory_space=pl.ANY)
SMEM = pl.BlockSpec(memory_space=pltpu.SMEM)
LAST = (((1,), (1,)), ((), ()))


def layer_norm(values, gain):
    floats = values.astype(F32)
    centre = jnp.mean(floats, axis=-1, keepdims=True)
    spread = jnp.mean(jnp.square(floats - centre), axis=-1, keepdims=True)
    inverse = lax.rsqrt(spread + EPSILON)
    normal = (floats - centre) * inverse
    return (normal * gain, normal, inverse)


def gelu_pair(values):
    c = 0.7978845608028654
    square = values * values
    tanh = jnp.tanh(c * values * (1.0 + 0.044715 * square))
    half = 0.5 * (1.0 + tanh)
    slope = half + 0.5 * values * (1.0 - tanh * tanh) * c * (1.0 + 3 * 0.044715 * square)
    return values * half, slope


def dot(a, b):
    return jnp.dot(a, b, preferred_element_type=F32)


def dot_last(a, b):
    return lax.dot_general(a, b, LAST, preferred_element_type=F32)


def block_copies(place, first, blocks, whole, sems):
    rows, cols = blocks[0].shape[0] // 2, blocks[0].shape[1]
    group = place[0]
    copies = []
    for bits, block in enumerate(blocks):
        source = block.at[pl.ds(first * rows, rows)]
        place_rows = pl.ds(pl.multiple_of((group ^ bits) * rows, 16), rows)
        if bits < 2:
            copies.append(pltpu.make_async_copy(source, whole.at[place_rows], sems.at[bits]))
            continue
        quarter = cols // PARTS
        for k in range(PARTS):
            start = pl.multiple_of(lax.rem(place[2] + k, PARTS) * quarter, 256)
            copies.append(
                pltpu.make_async_copy(
                    block.at[pl.ds(first * rows, rows), pl.ds(k * quarter, quarter)],
                    whole.at[place_rows, pl.ds(start, quarter)],
                    sems.at[PARTS * bits + k - 6],
                )
            )
    return copies


def up_kernel(
    place, image, gain, w0, w1, w2, w3, act, slope, in_rows, up, rows4, sems, row_sems
):
    weights = (w0, w1, w2, w3)
    copies = block_copies(place, 0, weights, up, sems)
    rows = in_rows.shape[0]
    moves = []
    for k in range(PARTS):
        start = pl.multiple_of(lax.rem(place[1] + PARTS - k, PARTS) * rows, 16)
        moves.append(
            pltpu.make_async_copy(
                image.at[pl.ds(start, rows)], rows4.at[pl.ds(k * rows, rows)], row_sems.at[k]
            )
        )
    for copy in moves + copies:
        copy.start()
    for copy in moves:
        copy.wait()
    in_rows[...] = rows4[pl.ds(0, rows)]
    normed = layer_norm(rows4[...], gain[...])[0].astype(BF)
    for copy in copies:
        copy.wait()
    for n in range(4):
        cols = pl.ds(n * 256, 256)
        value, grad = gelu_pair(dot(normed, up[:, cols]))
        act[:, cols] = value.astype(BF)
        slope[:, cols] = grad


def down_kernel(place, act, w0, w1, w2, w3, o0, o1, o2, o3, down, sems):
    weights = (w0, w1, w2, w3)
    copies = block_copies(place, 1, weights, down, sems)
    for copy in copies:
        copy.start()
    for copy in copies:
        copy.wait()
    split_rows(dot_last(act[...], down[...]).astype(BF), (o0, o1, o2, o3))


def split_rows(value, outs):
    rows = outs[0].shape[0]
    for k, out in enumerate(outs):
        out[...] = value[k * rows : (k + 1) * rows]


def query_kernel(caption, p0, p1, p2, p3, query, d_attn, w, sems):
    dec = caption.shape[-1]
    skip = p0.shape[1] - dec
    copies = [
        pltpu.make_async_copy(p.at[:, pl.ds(skip, dec)], w.at[k], sems.at[k])
        for k, p in enumerate((p0, p1, p2, p3))
    ]
    for copy in copies:
        copy.start()
    text, cot = caption[0], caption[1]
    for k, copy in enumerate(copies):
        copy.wait()
        query[k] = (dot_last(text, w[k, :HEAD_DIM]) * HEAD_DIM ** (-0.5)).astype(BF)
        d_attn[k] = dot_last(cot, w[k, HEAD_DIM:]).astype(BF)


def attention_kernel(
    e0, e1, e2, e3, query, d_attn, p0, p1, p2, p3, o0, o1, o2, o3, encoded, d_pair, w, sems
):
    width = e0.shape[1]
    copies = [
        pltpu.make_async_copy(p.at[:, pl.ds(0, width)], w.at[k], sems.at[k])
        for k, p in enumerate((p0, p1, p2, p3))
    ]
    for copy in copies:
        copy.start()
    rows = e0.shape[0]
    for k, e in enumerate((e0, e1, e2, e3)):
        encoded[pl.ds(k * rows, rows)] = e[...]
    tokens = encoded[...]
    term = None
    for k, copy in enumerate(copies):
        copy.wait()
        pair = dot_last(tokens, w[k]).astype(BF)
        keys, values = pair[:, :HEAD_DIM], pair[:, HEAD_DIM:]
        q, da = query[k], d_attn[k]
        scores = dot_last(keys, q)
        expo = jnp.exp(scores - jnp.max(scores, axis=0, keepdims=True))
        probs = expo / jnp.sum(expo, axis=0, keepdims=True)
        d_probs = dot_last(values, da)
        mean = jnp.sum(probs * d_probs, axis=0, keepdims=True)
        d_scores = (probs * (d_probs - mean)).astype(BF)
        d_keys = dot(d_scores, q).astype(BF)
        d_values = dot(probs.astype(BF), da).astype(BF)
        grads = jnp.concatenate([d_keys, d_values], axis=1)
        d_pair[:, pl.ds(k * 2 * HEAD_DIM, 2 * HEAD_DIM)] = grads
    for k in range(PARTS):
        part = dot(d_pair[:, pl.ds(k * 2 * HEAD_DIM, 2 * HEAD_DIM)], w[k])
        term = part if term is None else term + part
    split_rows(term.astype(BF), (o0, o1, o2, o3))


def back_kernel(
    place, g0, g1, g2, g3, slope, w0, w1, w2, w3,
    o0, o1, o2, o3, down, up, grads, d_pre, down_sems, up_sems,
):
    weights = (w0, w1, w2, w3)
    first = block_copies(place, 1, weights, down, down_sems)
    second = block_copies(place, 0, weights, up, up_sems)
    for copy in first + second:
        copy.start()
    rows = g0.shape[0]
    for k, g in enumerate((g0, g1, g2, g3)):
        grads[pl.ds(k * rows, rows)] = g[...]
    for copy in first:
        copy.wait()
    for n in range(4):
        cols = pl.ds(n * 256, 256)
        d_pre[:, cols] = (dot(grads[...], down[:, cols]) * slope[:, cols]).astype(BF)
    for copy in second:
        copy.wait()
    split_rows(dot_last(d_pre[...], up[...]).astype(BF), (o0, o1, o2, o3))


def shift(value, axis, by):
    size = lax.axis_size(axis)
    return lax.ppermute(value, axis, [(i, (i + by) % size) for i in range(size)])


def swap(value, axis, bit=1):
    size = lax.axis_size(axis)
    return lax.ppermute(value, axis, [(i, i ^ bit) for i in range(size)])


def rows_at(value, start, size):
    return lax.dynamic_slice_in_dim(value, start, size, axis=0)


def after(value, *others):
    return lax.optimization_barrier((value,) + others)[0]


def quarter_of(value, which, dim):
    quarter = value.shape[dim] // PARTS
    return lax.dynamic_slice_in_dim(value, which * quarter, quarter, axis=dim)


def send_blocks(blocks):
    return [blocks[0]] + [shift(blocks[PARTS - by], "tensor", by) for by in range(1, PARTS)]


def add_blocks(blocks):
    total = blocks[0].astype(F32)
    for block in blocks[1:]:
        total = total + block.astype(F32)
    return total


def gather_blocks(block):
    return [block] + [shift(block, "tensor", by) for by in range(1, PARTS)]


def local(
    image_in, enc_gain, enc_up, enc_down, text_in, query_gain, w_query, w_key, w_value, w_out, cotangent
):
    _, patches, width = image_in.shape
    group = lax.axis_index("yh") * 2 + lax.axis_index("core")
    tensor = lax.axis_index("tensor")
    flat_in = image_in.reshape(patches, width)
    rows = patches // PARTS
    hidden = enc_up.shape[1]
    dec = w_query.shape[0]
    shape = jax.ShapeDtypeStruct
    row_outs = [shape((rows, width), BF)] * PARTS
    gain = enc_gain.reshape(1, width)
    dma = pltpu.SemaphoreType.DMA

    which = lax.rem(lax.axis_index("x") + lax.axis_index("zl"), PARTS)
    piece = jnp.concatenate(
        [quarter_of(enc_up, which, 1), quarter_of(enc_down, which, 0).T], axis=0
    )
    place = jnp.stack([group, tensor, which]).astype(jnp.int32)
    piece = swap(piece, "yh")
    pieces = [piece, shift(piece, "x", -1), shift(piece, "x", 2), shift(piece, ("zh", "zl"), 1)]
    far = jnp.concatenate(pieces, axis=1)
    own = jnp.concatenate([enc_up, enc_down.T], axis=0)
    weights = (own, swap(own, "core"), far, swap(far, "core"))
    pair_own = jnp.concatenate([w_key, w_value], axis=1).T
    text_own = jnp.concatenate([w_query.T, w_out], axis=0)
    heads_own = jnp.concatenate([pair_own, text_own], axis=1)

    heads_piece = swap(quarter_of(after(heads_own, *pieces), lax.axis_index("x"), 0), "yh")
    heads_near = swap(after(heads_own, far), "core")

    text_normed = layer_norm(text_in, query_gain)[0].astype(BF)
    both = after(jnp.stack([text_normed, cotangent], axis=1), piece)
    sent = jnp.broadcast_to(both, (PARTS,) + both.shape).reshape((-1,) + both.shape[1:])
    caption = lax.all_to_all(sent, ("tensor", "yh", "core"), 0, 0, tiled=True)

    act, slope, in_rows = pl.pallas_call(
        up_kernel,
        name="encoder_up",
        out_shape=[shape((patches, hidden), BF), shape((patches, hidden), F32), row_outs[0]],
        in_specs=[SMEM, ANY, VMEM] + [ANY] * 4,
        out_specs=[VMEM] * 3,
        scratch_shapes=[
            pltpu.VMEM((width, hidden), BF),
            pltpu.VMEM((patches, width), BF),
            dma((COPIES,)),
            dma((PARTS,)),
        ],
        compiler_params=PARAMS,
    )(place, flat_in, gain, *weights)
    branch = pl.pallas_call(
        down_kernel,
        name="encoder_down",
        out_shape=row_outs,
        in_specs=[SMEM, VMEM] + [ANY] * 4,
        out_specs=[VMEM] * PARTS,
        scratch_shapes=[pltpu.VMEM((width, hidden), BF), dma((COPIES,))],
        compiler_params=PARAMS,
    )(place, act, *weights)
    heads_far = lax.all_gather(after(heads_piece, act), "x", axis=0, tiled=True)
    branch = list(branch)
    branch[1], caption = lax.optimization_barrier((branch[1], caption))
    caption = jnp.swapaxes(caption, 0, 1).reshape(2, -1, dec)
    encoded_rows = (in_rows.astype(F32) + add_blocks(send_blocks(branch))).astype(BF)
    encoded_blocks = gather_blocks(encoded_rows)

    heads = (heads_own, heads_near, heads_far, swap(after(heads_far, encoded_rows), "core"))

    head_shape = shape((4, caption.shape[1], HEAD_DIM), BF)
    query, d_attn = pl.pallas_call(
        query_kernel,
        name="query",
        out_shape=[head_shape, head_shape],
        in_specs=[VMEM] + [ANY] * 4,
        out_specs=[VMEM] * 2,
        scratch_shapes=[pltpu.VMEM((4, 2 * HEAD_DIM, dec), BF), dma((4,))],
        compiler_params=PARAMS,
    )(caption, *heads)
    *term, encoded, d_pair = pl.pallas_call(
        attention_kernel,
        name="attention",
        out_shape=row_outs + [shape((patches, width), BF), shape((patches, 8 * HEAD_DIM), BF)],
        in_specs=[VMEM] * 6 + [ANY] * 4,
        out_specs=[VMEM] * 6,
        scratch_shapes=[pltpu.VMEM((4, 2 * HEAD_DIM, width), BF), dma((4,))],
        compiler_params=PARAMS,
    )(*encoded_blocks, query, d_attn, *heads)
    term_blocks = send_blocks(term)
    grad_rows = add_blocks(term_blocks).astype(BF)
    grad_blocks = gather_blocks(grad_rows)

    pair_cols = 2 * HEAD_DIM
    cols = [d_pair[:, k * pair_cols : (k + 1) * pair_cols] for k in range(4)]
    contract = (((0,), (0,)), ((), ()))
    give = lax.dot_general(
        encoded, jnp.concatenate([cols[1], cols[3]], axis=1), contract, preferred_element_type=F32
    ).astype(BF)
    later = [after(cols[0], grad_rows), after(cols[2], grad_rows)]
    keep = lax.dot_general(
        encoded, jnp.concatenate(later, axis=1), contract, preferred_element_type=F32
    )
    sums = (keep + swap(give, "core").astype(F32)).astype(BF)
    sums = lax.psum_scatter(sums, "x", scatter_dimension=0, tiled=True)

    d_norm = pl.pallas_call(
        back_kernel,
        name="encoder_back",
        out_shape=row_outs,
        in_specs=[SMEM] + [VMEM] * 5 + [ANY] * 4,
        out_specs=[VMEM] * PARTS,
        scratch_shapes=[
            pltpu.VMEM((width, hidden), BF),
            pltpu.VMEM((width, hidden), BF),
            pltpu.VMEM((patches, width), BF),
            pltpu.VMEM((patches, hidden), BF),
            dma((COPIES,)),
            dma((COPIES,)),
        ],
        compiler_params=PARAMS,
    )(place, *grad_blocks, slope, *weights)
    d_norm = list(d_norm)
    d_norm[1], sums = lax.optimization_barrier((d_norm[1], sums))
    sums = lax.all_to_all(sums.reshape(8, -1, 2 * pair_cols), ("zh", "zl"), 0, 0, tiled=True)
    d_normed = add_blocks(send_blocks(d_norm))
    _, normal, inverse = layer_norm(in_rows, enc_gain)
    scaled_grad = d_normed * enc_gain
    d_input = inverse * (
        scaled_grad
        - jnp.mean(scaled_grad, axis=-1, keepdims=True)
        - normal * jnp.mean(scaled_grad * normal, axis=-1, keepdims=True)
    )
    image_rows = (grad_rows.astype(F32) + d_input).astype(BF)
    image_grad = lax.all_gather(image_rows, "tensor", axis=0, tiled=True).reshape(1, patches, width)
    image_grad, sums = lax.optimization_barrier((image_grad, sums))
    sums = jnp.sum(sums.astype(F32), axis=0)
    sums = sums[:, :pair_cols] + swap(sums[:, pair_cols:].astype(BF), "yh").astype(F32)
    key_grad, value_grad = sums[:, :HEAD_DIM], sums[:, HEAD_DIM:]
    return (image_grad, key_grad, value_grad)


def solution(mesh):
    fine = Mesh(
        mesh.devices.reshape(4, 2, 4, 4, 2, 2), ("x", "zh", "zl", "tensor", "yh", "core")
    )
    dp, group, heads = ("x", "zh", "zl"), ("yh", "core"), ("tensor", "yh", "core")
    in_specs = (
        P(dp + group, None, None),
        P(),
        P(group, "tensor"),
        P("tensor", group),
        P(dp, heads, None),
        P(),
        P(None, heads),
        P(None, heads),
        P(None, heads),
        P(heads, None),
        P(dp, heads, None),
    )
    out_specs = (P(dp + group, None, None), P(dp, heads), P(dp, heads))
    return jax.shard_map(local, mesh=fine, in_specs=in_specs, out_specs=out_specs, check_vma=False)
```
